128 devices in a mesh: sec: 2 (over z_lo), dev: 64 (over z_hi, x, y, core).
Axes of the slice: x: 4, y: 4, z: 4 (z_hi: 2, z_lo: 2; z = z_hi * 2 + z_lo), core: 2. Of those that a mesh axis runs over, the one named last changes fastest.
Arguments:
- hidden: bfloat16 [1024, 7168], P(('sec', 'dev')), may hold values from -40 to 40
- norm_gain: float32 [7168], replicated, may hold values from 0.1 to 1.9
- routes: int32 [1024, 8], P(('sec', 'dev')), may hold values from 0 to 31, as said below
- gate_values: float32 [1024, 8], P(('sec', 'dev')), may hold values from 0.1 to 0.6
- w_gate: bfloat16 [7168, 65536], P(None, ('sec', 'dev')), may hold values from -0.0625 to 0.0625
- w_up: bfloat16 [7168, 65536], P(None, ('sec', 'dev')), may hold values from -0.0625 to 0.0625
- w_down: bfloat16 [65536, 7168], P(('sec', 'dev')), may hold values from -0.125 to 0.125
- queries: bfloat16 [128, 128, 576], P(('sec', 'dev')), may hold values from -80 to 80
- latent_cache: bfloat16 [128, 1536, 576], P(('sec', 'dev')), may hold values from -6 to 6
- lengths: int32 [128], P(('sec', 'dev')), may hold values from 2 to 1536, as said below
Outputs:
- moe_out: bfloat16 [1024, 7168], P(('sec', 'dev'))
- attn_out: bfloat16 [128, 128, 512], P(('sec', 'dev'))
The draws below stay inside these ranges and needn't reach their ends.
Inputs may be any that keep to these rules, and one draw needn't show every extreme that they name: `routes`: each row names 8 different experts. Among the 8 rows of one device no expert is named more than 4 times, and one expert, the same for every device, is named exactly 4 times by the rows of each device. `lengths`: every row keeps its first two positions; some rows use all 1536.
All inputs are finite; a program needn't handle non-finite values.
Results may differ from the reference program's by a relative error of at most 0.013.
Values may be sent and summed in bfloat16 or wider, within the bound.
No kernel may reach another device: no remote copies, remote signals or barrier semaphores. Data moves between devices by JAX's collectives and lax.ppermute only.
A program may use at most 128 MiB of HBM per device.

```python
import math
import jax
import jax.numpy as jnp
from jax import lax

D = 7168
FF = 2048
H = 128
LAT = 512
ROPE = 64
TOPK = 8
EXPERTS = 32
CTX = 1536
TOK_DEV = 8
CAP = 4
TOKENS = 1024
AROWS = 128
N_SEC = 2
N_DEV = 64


def lead_positions(key):
    normal_part = jnp.clip(jax.random.normal(jax.random.fold_in(key, 1), (AROWS, 2, LAT + ROPE)), -6.0, 6.0)
    drawn = normal_part
    half_lat = LAT // 2
    first_key = drawn[:, 0]
    second_key = drawn[:, 1]
    tied_key = second_key.at[:, :half_lat].set(second_key[:, :half_lat])
    return jnp.stack([first_key, tied_key], axis=1)


def draw_latent_cache(key, part):
    lead_keys = lead_positions(key)
    key = jax.random.fold_in(key, 21)
    other_keys = jnp.clip(jax.random.normal(key, (AROWS, CTX - 2, LAT + ROPE)), -6.0, 6.0)
    return jnp.concatenate([lead_keys, other_keys], axis=1).astype(jnp.bfloat16)


def draw_queries(key, part):
    key = jax.random.fold_in(key, 31)
    result = jnp.clip(jax.random.normal(key, (AROWS, H, LAT + ROPE)), -6.0, 6.0)
    return result.astype(jnp.bfloat16)


def draw_lengths(key, part):
    key = jax.random.fold_in(key, 41)
    long_rows = jax.random.randint(jax.random.fold_in(key, 1), (AROWS,), 0, 8) == 0
    short_len = jax.random.randint(jax.random.fold_in(key, 2), (AROWS,), 2, CTX // 4 + 1)
    chosen_len = jnp.where(long_rows, CTX, short_len)
    return chosen_len.at[0].set(CTX).astype(jnp.int32)


def draw_hidden(key, part):
    key = jax.random.fold_in(key, 51)
    row_scale = jnp.exp(jax.random.uniform(jax.random.fold_in(key, 1), (TOKENS, 1)) * math.log(10.0))
    col_scale = jnp.exp(jax.random.uniform(jax.random.fold_in(key, 2), (1, D)) * math.log(10.0))
    drawn = jnp.clip(jax.random.normal(jax.random.fold_in(key, 3), (TOKENS, D)), -4.0, 4.0)
    return (0.1 * drawn * row_scale * col_scale).astype(jnp.bfloat16)


def draw_routes(key, part):
    key = jax.random.fold_in(key, 61)
    shuffled = jax.random.permutation(jax.random.fold_in(key, 0), EXPERTS).astype(jnp.int32)
    hot_expert = shuffled[0]
    other_experts = shuffled[1:]
    block_count = TOKENS // TOK_DEV
    slot_index = jnp.arange(TOPK, dtype=jnp.int32)

    def one_block(block_no):
        block_key = jax.random.fold_in(key, block_no + 1)
        row_perm = jax.random.permutation(jax.random.fold_in(block_key, 1), TOK_DEV).astype(jnp.int32)
        row_rank = jnp.argsort(row_perm).astype(jnp.int32)
        is_hot = (row_rank < CAP).astype(jnp.int32)
        block_others = other_experts[jax.random.permutation(jax.random.fold_in(block_key, 2), EXPERTS - 1)]
        offset = jax.random.randint(jax.random.fold_in(block_key, 3), (), 0, EXPERTS - 1)
        used_count = TOPK - is_hot
        consumed = jnp.cumsum(used_count) - used_count
        list_index = consumed[:, None] + slot_index[None, :] - is_hot[:, None]
        listed = block_others[(offset + list_index) % (EXPERTS - 1)]
        row_ids = jnp.where((slot_index[None, :] == 0) & (is_hot[:, None] == 1), hot_expert, listed)
        rotation = jax.random.randint(jax.random.fold_in(block_key, 4), (TOK_DEV,), 0, TOPK)
        column_index = (slot_index[None, :] + rotation[:, None]) % TOPK
        return jnp.take_along_axis(row_ids, column_index, axis=1)
    blocks_all = jax.vmap(one_block)(jnp.arange(block_count))
    return blocks_all.reshape(TOKENS, TOPK).astype(jnp.int32)


def levels(key, extent, split, low, largest):
    gain = 1.0
    for dim, parts in split:
        steps = jax.random.uniform(jax.random.fold_in(jax.random.fold_in(key, 6), dim), (parts,), jnp.float32, low / len(split), largest / len(split))
        gain = gain * jnp.repeat(jnp.exp(steps), extent[dim] // parts).reshape((-1,) + (1,) * (len(extent) - 1 - dim))
    return gain


def gaussian(stream_key, dims, deviation, reach, cuts=(), kind=jnp.bfloat16):
    values = jax.random.normal(stream_key, dims, jnp.float32) * deviation
    if len(cuts) > 0:
        values = levels(stream_key, dims, cuts, -0.22, 0.18) * values
    return jnp.clip(values, min=-reach, max=reach).astype(kind)


def setup_inputs(seed: int = 0) -> dict:
    keys = jax.random.split(jax.random.key(seed), 11)
    hidden = draw_hidden(jax.random.fold_in(keys[10], 71), 0)
    norm_gain = jnp.clip(1.0 + 0.18 * jax.random.normal(keys[1], (D,), jnp.float32), 0.1, 1.9)
    routes = draw_routes(jax.random.fold_in(keys[10], 71), 0)
    gate_values = jnp.clip(jnp.exp(math.log(0.6) - 1.7917595 * jax.random.uniform(keys[3], (TOKENS, TOPK), jnp.float32) ** levels(keys[3], (TOKENS, TOPK), ((0, 128),), -0.2, 0.2)), 0.1, 0.6)
    w_gate = gaussian(keys[4], (D, EXPERTS * FF), D ** -0.5, 0.0625, ((1, 128),))
    w_up = gaussian(keys[5], (D, EXPERTS * FF), D ** -0.5, 0.0625, ((1, 128),))
    w_down = gaussian(keys[6], (EXPERTS * FF, D), FF ** -0.5, 0.125, ((0, 128),))
    queries = draw_queries(jax.random.fold_in(keys[10], 71), 0)
    latent_cache = draw_latent_cache(jax.random.fold_in(keys[10], 71), 0)
    lengths = draw_lengths(jax.random.fold_in(keys[10], 71), 0)
    return {"hidden": hidden, "norm_gain": norm_gain, "routes": routes, "gate_values": gate_values, "w_gate": w_gate, "w_up": w_up, "w_down": w_down, "queries": queries, "latent_cache": latent_cache, "lengths": lengths}


norm_eps = 1e-06
score_scale = 0.07216878364870322

def attend(queries, latent_cache, lengths):
    scores = jnp.einsum('rhk,rck->rhc', queries.astype(jnp.float32), latent_cache.astype(jnp.float32), precision=lax.Precision.HIGHEST) * score_scale
    in_range = jnp.arange(CTX)[None, None, :] < lengths[:, None, None]
    scores = jnp.where(in_range, scores, -jnp.inf)
    row_max = lax.optimization_barrier(jnp.max(scores, axis=-1, keepdims=True))
    raised = jnp.exp(scores - row_max)
    probs = (raised / lax.optimization_barrier(jnp.sum(raised, axis=-1, keepdims=True))).astype(jnp.bfloat16)
    attended = jnp.einsum('rhc,rcl->rhl', probs.astype(jnp.float32), latent_cache[:, :, :LAT].astype(jnp.float32), precision=lax.Precision.HIGHEST)
    return attended.astype(jnp.bfloat16)

def reference(hidden, norm_gain, routes, gate_values, w_gate, w_up, w_down, queries, latent_cache, lengths):
    attn_out = attend(queries, latent_cache, lengths)
    features = hidden.astype(jnp.float32)
    squares = lax.optimization_barrier(jnp.mean(features * features, axis=-1, keepdims=True))
    normed = (features * lax.rsqrt(squares + norm_eps) * norm_gain).astype(jnp.bfloat16)
    group_size = N_SEC * N_DEV // EXPERTS
    unit_count = FF // group_size
    most_rows = TOKENS // TOK_DEV * CAP

    def one_expert(running, expert):
        chosen = routes == expert
        is_taken = jnp.any(chosen, axis=1)
        weight = lax.optimization_barrier(jnp.sum(jnp.where(chosen, gate_values, 0.0), axis=1))
        row_order = jnp.argsort(jnp.where(is_taken, 0, 1).astype(jnp.int32), stable=True)[:most_rows].astype(jnp.int32)
        gathered = normed[row_order]
        column_start = (expert * FF).astype(jnp.int32)
        gate_cols = lax.dynamic_slice_in_dim(w_gate, column_start, FF, 1)
        up_cols = lax.dynamic_slice_in_dim(w_up, column_start, FF, 1)
        down_rows = lax.dynamic_slice_in_dim(w_down, column_start, FF, 0)
        gate_part = jnp.dot(gathered, gate_cols, preferred_element_type=jnp.float32)
        up_part = jnp.dot(gathered, up_cols, preferred_element_type=jnp.float32)
        hidden_act = (jax.nn.silu(gate_part) * up_part).astype(jnp.bfloat16)
        pieces = jnp.einsum('mgf,gfd->gmd', hidden_act.reshape(most_rows, group_size, unit_count).astype(jnp.float32), down_rows.reshape(group_size, unit_count, D).astype(jnp.float32), precision=lax.Precision.HIGHEST)
        rounded = lax.optimization_barrier(pieces.astype(jnp.bfloat16))
        expert_sum = lax.optimization_barrier(jnp.sum(rounded.astype(jnp.float32), axis=0))
        factor = jnp.where(is_taken, weight, 0.0)[row_order]
        return (running.at[row_order].add(expert_sum * factor[:, None]), None)
    running, _ = lax.scan(one_expert, jnp.zeros((TOKENS, D), jnp.float32), jnp.arange(EXPERTS, dtype=jnp.int32))
    return (running.astype(jnp.bfloat16), attn_out)
```

```python
import jax
import jax.numpy as jnp
from jax import lax
from jax.experimental import pallas as pl
from jax.experimental.pallas import tpu as pltpu
from jax.sharding import Mesh, PartitionSpec as P

LAT = 512
EXPERTS = 32
CAP = 4

AXES = ("zl", "zh", "x", "y", "core")
SIZES = (2, 2, 4, 4, 2)
CHIPS = ("zl", "zh", "x", "y")
N_CHIPS = 64
QUARTERS = 4
BLOCK = CAP * QUARTERS
ROWS = N_CHIPS * BLOCK
STEP = 256

norm_eps = 1e-06
score_scale = 0.07216878364870322


def slot_matches(routes, lanes):
    rows = routes.shape[0]
    packed_row = lax.broadcasted_iota(jnp.int32, (rows, lanes), 1)
    expert = packed_row // (2 * BLOCK)
    slot = packed_row % CAP
    piece = (packed_row // CAP) % QUARTERS
    named = jnp.zeros((rows, lanes), jnp.bool_)
    for k in range(routes.shape[1]):
        named = named | (routes[:, k : k + 1] == expert)
    before = (
        lax.broadcasted_iota(jnp.int32, (rows, rows), 0)
        > lax.broadcasted_iota(jnp.int32, (rows, rows), 1)
    ).astype(jnp.float32)
    rank = jnp.dot(before, named.astype(jnp.float32), preferred_element_type=jnp.float32)
    return expert, piece, named & (rank == slot.astype(jnp.float32))


def pack_kernel(hidden_ref, gain_ref, routes_ref, send_ref):
    features = hidden_ref[...].astype(jnp.float32)
    squares = jnp.mean(features * features, axis=-1, keepdims=True)
    normed = features * lax.rsqrt(squares + norm_eps) * gain_ref[...]
    width = send_ref.shape[1]
    stacked = jnp.concatenate(
        [normed[:, q * width : (q + 1) * width] for q in range(QUARTERS)], axis=0
    ).astype(jnp.bfloat16)
    _, piece, match = slot_matches(routes_ref[...], send_ref.shape[0])
    picked = jnp.concatenate(
        [(match & (piece == q)).astype(jnp.float32) for q in range(QUARTERS)], axis=0
    ).astype(jnp.bfloat16)
    for start in range(0, send_ref.shape[0], STEP):
        send_ref[start : start + STEP, :] = lax.dot_general(
            picked[:, start : start + STEP],
            stacked,
            (((0,), (0,)), ((), ())),
            preferred_element_type=jnp.float32,
        ).astype(jnp.bfloat16)


def pack(hidden, norm_gain, routes):
    width = hidden.shape[1] // QUARTERS
    return pl.pallas_call(
        pack_kernel,
        out_shape=jax.ShapeDtypeStruct((ROWS, width), jnp.bfloat16),
        compiler_params=pltpu.CompilerParams(vmem_limit_bytes=24 * 2**20),
        name="pack_rows",
    )(hidden, norm_gain.reshape(1, -1), routes)


def ungroup_matrix():
    to = lax.broadcasted_iota(jnp.int32, (STEP, STEP), 0)
    frm = lax.broadcasted_iota(jnp.int32, (STEP, STEP), 1)
    per_piece = STEP // QUARTERS
    want = ((to % per_piece) // CAP) * BLOCK + (to // per_piece) * CAP + to % CAP
    return (frm == want).astype(jnp.float32).astype(jnp.bfloat16)


def gate_up_kernel(rows_ref, gate_ref, up_ref, act_ref, gate_acc, up_acc, order):
    step = pl.program_id(0)

    @pl.when(step == 0)
    def _():
        gate_acc[...] = jnp.zeros_like(gate_acc)
        up_acc[...] = jnp.zeros_like(up_acc)
        order[...] = ungroup_matrix()

    per_piece = STEP // QUARTERS
    parts = []
    for start in range(0, ROWS, STEP):
        moved = jnp.dot(
            order[...], rows_ref[start : start + STEP, :], preferred_element_type=jnp.float32
        ).astype(jnp.bfloat16)
        parts.append(
            jnp.concatenate(
                [moved[q * per_piece : (q + 1) * per_piece] for q in range(QUARTERS)], axis=1
            )
        )
    rows = jnp.concatenate(parts, axis=0)
    depth = rows.shape[1]
    units = gate_acc.shape[1]
    gate_acc[...] += jnp.dot(
        rows, gate_ref[...].reshape(depth, units), preferred_element_type=jnp.float32
    )
    up_acc[...] += jnp.dot(
        rows, up_ref[...].reshape(depth, units), preferred_element_type=jnp.float32
    )

    @pl.when(step == pl.num_programs(0) - 1)
    def _():
        gate = gate_acc[...]
        act_ref[...] = (gate / (1.0 + jnp.exp(-gate)) * up_acc[...]).astype(jnp.bfloat16)


def gate_up(packed, w_gate, w_up):
    width = packed.shape[1]
    units = w_gate.shape[1]
    weight_spec = pl.BlockSpec((QUARTERS, STEP, units), lambda j: (0, j, 0))
    flops = 2 * 2 * (ROWS // QUARTERS) * w_gate.size
    return pl.pallas_call(
        gate_up_kernel,
        grid=(width // STEP,),
        in_specs=[pl.BlockSpec((ROWS, STEP), lambda j: (0, j)), weight_spec, weight_spec],
        out_specs=pl.BlockSpec((ROWS // QUARTERS, units), lambda j: (0, 0)),
        out_shape=jax.ShapeDtypeStruct((ROWS // QUARTERS, units), jnp.bfloat16),
        scratch_shapes=[
            pltpu.VMEM((ROWS // QUARTERS, units), jnp.float32),
            pltpu.VMEM((ROWS // QUARTERS, units), jnp.float32),
            pltpu.VMEM((STEP, STEP), jnp.bfloat16),
        ],
        compiler_params=pltpu.CompilerParams(vmem_limit_bytes=24 * 2**20),
        cost_estimate=pl.CostEstimate(
            flops=flops, bytes_accessed=2 * (2 * w_gate.size + packed.size), transcendentals=0
        ),
        name="gate_up",
    )(
        packed,
        w_gate.reshape(QUARTERS, width, units),
        w_up.reshape(QUARTERS, width, units),
    )


def down_kernel(act_ref, *refs):
    weights = refs[:QUARTERS]
    other = refs[QUARTERS] if len(refs) == QUARTERS + 3 else None
    out_ref, order = refs[-2:]

    @pl.when(pl.program_id(0) == 0)
    def _():
        order[...] = ungroup_matrix()

    per_piece = STEP // QUARTERS
    parts = [
        jnp.dot(act_ref[...], w[...], preferred_element_type=jnp.float32).astype(jnp.bfloat16)
        for w in weights
    ]
    for index in range(ROWS // STEP):
        grouped = jnp.concatenate(
            [part[index * per_piece : (index + 1) * per_piece] for part in parts], axis=0
        )
        moved = lax.dot_general(
            order[...], grouped, (((0,), (0,)), ((), ())), preferred_element_type=jnp.float32
        )
        here = slice(index * STEP, (index + 1) * STEP)
        if other is not None:
            moved = moved + other[here, :].astype(jnp.float32)
        out_ref[here, :] = moved.astype(jnp.bfloat16)


def down(act, w_down, other=None):
    units, model_width = w_down.shape
    width = model_width // QUARTERS
    steps = width // STEP
    packed_spec = pl.BlockSpec((ROWS, STEP), lambda j: (0, j))
    weight_specs = [
        pl.BlockSpec((units, STEP), lambda j, q=q: (0, q * steps + j)) for q in range(QUARTERS)
    ]
    extra = [] if other is None else [other]
    return pl.pallas_call(
        down_kernel,
        grid=(steps,),
        in_specs=[pl.BlockSpec(act.shape, lambda j: (0, 0))]
        + weight_specs
        + [packed_spec] * len(extra),
        out_specs=packed_spec,
        out_shape=jax.ShapeDtypeStruct((ROWS, width), jnp.bfloat16),
        scratch_shapes=[pltpu.VMEM((STEP, STEP), jnp.bfloat16)],
        compiler_params=pltpu.CompilerParams(vmem_limit_bytes=24 * 2**20),
        cost_estimate=pl.CostEstimate(
            flops=2 * act.shape[0] * w_down.size,
            bytes_accessed=2 * (w_down.size + (1 + len(extra)) * ROWS * width),
            transcendentals=0,
        ),
        name="down",
    )(act, *([w_down] * QUARTERS), *extra)


def combine_kernel(rows_ref, routes_ref, gates_ref, out_ref, weigh):
    step = pl.program_id(0)
    tok_rows = routes_ref.shape[0]

    @pl.when(step == 0)
    def _():
        routes = routes_ref[...]
        gates = gates_ref[...]
        expert, piece, match = slot_matches(routes, rows_ref.shape[0])
        gate = jnp.zeros(expert.shape, jnp.float32)
        for k in range(routes.shape[1]):
            gate = gate + jnp.where(routes[:, k : k + 1] == expert, gates[:, k : k + 1], 0.0)
        spread = jnp.concatenate(
            [jnp.where(match & (piece == q), gate, 0.0) for q in range(QUARTERS)], axis=0
        )
        high = spread.astype(jnp.bfloat16)
        low = spread - high.astype(jnp.float32)
        weigh[...] = jnp.concatenate([high.astype(jnp.float32), low], axis=0).astype(jnp.bfloat16)

    half = QUARTERS * tok_rows
    width = out_ref.shape[1] // QUARTERS
    both = jnp.dot(weigh[...], rows_ref[...], preferred_element_type=jnp.float32)
    total = (both[:half] + both[half:]).astype(jnp.bfloat16)
    for q in range(QUARTERS):
        columns = pl.ds(pl.multiple_of(q * width + step * STEP, STEP), STEP)
        out_ref[:, columns] = total[q * tok_rows : (q + 1) * tok_rows]


def combine(returned, routes, gate_values):
    width = returned.shape[1]
    tok_rows = routes.shape[0]
    return pl.pallas_call(
        combine_kernel,
        grid=(width // STEP,),
        in_specs=[
            pl.BlockSpec((ROWS, STEP), lambda j: (0, j)),
            pl.BlockSpec(routes.shape, lambda j: (0, 0)),
            pl.BlockSpec(gate_values.shape, lambda j: (0, 0)),
        ],
        out_specs=pl.BlockSpec((tok_rows, width * QUARTERS), lambda j: (0, 0)),
        out_shape=jax.ShapeDtypeStruct((tok_rows, width * QUARTERS), jnp.bfloat16),
        scratch_shapes=[pltpu.VMEM((2 * QUARTERS * tok_rows, ROWS), jnp.bfloat16)],
        compiler_params=pltpu.CompilerParams(vmem_limit_bytes=24 * 2**20),
        name="combine",
    )(returned, routes, gate_values)


def attend(queries, latent_cache, lengths):
    scores = (
        jnp.einsum("rhk,rck->rhc", queries, latent_cache, preferred_element_type=jnp.float32)
        * score_scale
    )
    in_range = jnp.arange(latent_cache.shape[1])[None, None, :] < lengths[:, None, None]
    scores = jnp.where(in_range, scores, -jnp.inf)
    row_max = jnp.max(scores, axis=-1, keepdims=True)
    raised = jnp.exp(scores - row_max)
    probs = (raised / jnp.sum(raised, axis=-1, keepdims=True)).astype(jnp.bfloat16)
    attended = jnp.einsum(
        "rhc,rcl->rhl", probs, latent_cache[:, :, :LAT], preferred_element_type=jnp.float32
    )
    return attended.astype(jnp.bfloat16)


def to_other_core(rows):
    return lax.ppermute(rows, "core", [(0, 1), (1, 0)])


def between_chips(rows):
    return lax.all_to_all(rows, CHIPS, split_axis=0, concat_axis=0, tiled=True)


def shards(
    hidden, norm_gain, routes, gate_values, w_gate, w_up, w_down, queries, latent_cache, lengths
):
    sent = pack(hidden, norm_gain, routes)
    own_rows = between_chips(sent)
    other_rows = to_other_core(own_rows)
    own_act = gate_up(own_rows, w_gate, w_up)
    other_act = gate_up(other_rows, w_gate, w_up)
    for_other = down(other_act, w_down)
    from_other = to_other_core(for_other)
    summed = down(own_act, w_down, from_other)
    returned = between_chips(summed)
    attn_out = attend(queries, latent_cache, lengths)
    moe_out = combine(returned, routes, gate_values)
    return (moe_out, attn_out)


def solution(mesh):
    fine = Mesh(mesh.devices.reshape(SIZES), AXES)
    placed = (
        P(AXES, None),
        P(),
        P(AXES, None),
        P(AXES, None),
        P(None, AXES),
        P(None, AXES),
        P(AXES, None),
        P(AXES, None, None),
        P(AXES, None, None),
        P(AXES),
    )
    return jax.shard_map(
        shards,
        mesh=fine,
        in_specs=placed,
        out_specs=(P(AXES, None), P(AXES, None, None)),
        check_vma=False,
    )
```

```python
import jax
import jax.numpy as jnp
from jax import lax
from jax.experimental import pallas as pl
from jax.experimental.pallas import tpu as pltpu
from jax.sharding import Mesh, PartitionSpec as P

LAT = 512
EXPERTS = 32
CAP = 4

AXES = ("zl", "zh", "x", "y", "core")
SIZES = (2, 2, 4, 4, 2)
CHIPS = ("zl", "zh", "x", "y")
N_CHIPS = 64
QUARTERS = 4
BLOCK = CAP * QUARTERS
ROWS = N_CHIPS * BLOCK
STEP = 256

norm_eps = 1e-06
score_scale = 0.07216878364870322


def slot_matches(routes, lanes):
    rows = routes.shape[0]
    packed_row = lax.broadcasted_iota(jnp.int32, (rows, lanes), 1)
    expert = packed_row // (2 * BLOCK)
    slot = packed_row % CAP
    piece = (packed_row // CAP) % QUARTERS
    named = jnp.zeros((rows, lanes), jnp.bool_)
    for k in range(routes.shape[1]):
        named = named | (routes[:, k : k + 1] == expert)
    before = (
        lax.broadcasted_iota(jnp.int32, (rows, rows), 0)
        > lax.broadcasted_iota(jnp.int32, (rows, rows), 1)
    ).astype(jnp.float32)
    rank = jnp.dot(before, named.astype(jnp.float32), preferred_element_type=jnp.float32)
    return expert, piece, named & (rank == slot.astype(jnp.float32))


def pack_kernel(hidden_ref, gain_ref, routes_ref, send_ref):
    features = hidden_ref[...].astype(jnp.float32)
    squares = jnp.mean(features * features, axis=-1, keepdims=True)
    normed = features * lax.rsqrt(squares + norm_eps) * gain_ref[...]
    width = send_ref.shape[1]
    stacked = jnp.concatenate(
        [normed[:, q * width : (q + 1) * width] for q in range(QUARTERS)], axis=0
    ).astype(jnp.bfloat16)
    _, piece, match = slot_matches(routes_ref[...], send_ref.shape[0])
    picked = jnp.concatenate(
        [(match & (piece == q)).astype(jnp.float32) for q in range(QUARTERS)], axis=0
    ).astype(jnp.bfloat16)
    for start in range(0, send_ref.shape[0], STEP):
        send_ref[start : start + STEP, :] = lax.dot_general(
            picked[:, start : start + STEP],
            stacked,
            (((0,), (0,)), ((), ())),
            preferred_element_type=jnp.float32,
        ).astype(jnp.bfloat16)


def pack(hidden, norm_gain, routes):
    width = hidden.shape[1] // QUARTERS
    return pl.pallas_call(
        pack_kernel,
        out_shape=jax.ShapeDtypeStruct((ROWS, width), jnp.bfloat16),
        compiler_params=pltpu.CompilerParams(vmem_limit_bytes=24 * 2**20),
        name="pack_rows",
    )(hidden, norm_gain.reshape(1, -1), routes)


def gate_up_kernel(rows_ref, gate_ref, up_ref, act_ref, rows):
    width = rows_ref.shape[1]
    slots = ROWS // QUARTERS
    for start in range(0, width, STEP):
        blocks = rows_ref[:, start : start + STEP].reshape(N_CHIPS, BLOCK, STEP)
        for q in range(QUARTERS):
            rows[:, q * width + start : q * width + start + STEP] = blocks[
                :, q * CAP : (q + 1) * CAP, :
            ].reshape(slots, STEP)
    gate = jnp.dot(rows[...], gate_ref[...], preferred_element_type=jnp.float32)
    up = jnp.dot(rows[...], up_ref[...], preferred_element_type=jnp.float32)
    act_ref[...] = (gate / (1.0 + jnp.exp(-gate)) * up).astype(jnp.bfloat16)


def gate_up(packed, w_gate, w_up):
    in_vmem = pl.BlockSpec(memory_space=pltpu.VMEM)
    slots = ROWS // QUARTERS
    depth, units = w_gate.shape
    return pl.pallas_call(
        gate_up_kernel,
        in_specs=[in_vmem] * 3,
        out_specs=in_vmem,
        out_shape=jax.ShapeDtypeStruct((slots, units), jnp.bfloat16),
        scratch_shapes=[pltpu.VMEM((slots, depth), jnp.bfloat16)],
        compiler_params=pltpu.CompilerParams(vmem_limit_bytes=12 * 2**20),
        cost_estimate=pl.CostEstimate(
            flops=2 * 2 * slots * w_gate.size,
            bytes_accessed=2 * (2 * w_gate.size + packed.size),
            transcendentals=0,
        ),
        name="gate_up",
    )(packed, w_gate, w_up)


def down_kernel(near_act_ref, far_act_ref, near_ref, far_ref, out_ref):
    width = out_ref.shape[1]
    for start in range(0, width, STEP):
        pieces = []
        for q in range(QUARTERS):
            columns = slice(q * width + start, q * width + start + STEP)
            piece = jnp.dot(
                near_act_ref[...], near_ref[:, columns], preferred_element_type=jnp.float32
            ) + jnp.dot(far_act_ref[...], far_ref[:, columns], preferred_element_type=jnp.float32)
            pieces.append(piece.reshape(N_CHIPS, CAP, STEP))
        out_ref[:, start : start + STEP] = (
            jnp.concatenate(pieces, axis=1).reshape(ROWS, STEP).astype(jnp.bfloat16)
        )


def down(near_act, far_act, near, far):
    in_vmem = pl.BlockSpec(memory_space=pltpu.VMEM)
    width = near.shape[1] // QUARTERS
    return pl.pallas_call(
        down_kernel,
        in_specs=[in_vmem] * 4,
        out_specs=in_vmem,
        out_shape=jax.ShapeDtypeStruct((ROWS, width), jnp.bfloat16),
        compiler_params=pltpu.CompilerParams(vmem_limit_bytes=12 * 2**20),
        cost_estimate=pl.CostEstimate(
            flops=2 * 2 * near_act.shape[0] * near.size,
            bytes_accessed=2 * (2 * near.size + ROWS * width),
            transcendentals=0,
        ),
        name="down",
    )(near_act, far_act, near, far)


def weigh_kernel(routes_ref, gates_ref, weigh_ref):
    routes = routes_ref[...]
    gates = gates_ref[...]
    expert, piece, match = slot_matches(routes, weigh_ref.shape[1])
    gate = jnp.zeros(expert.shape, jnp.float32)
    for k in range(routes.shape[1]):
        gate = gate + jnp.where(routes[:, k : k + 1] == expert, gates[:, k : k + 1], 0.0)
    spread = jnp.concatenate(
        [jnp.where(match & (piece == q), gate, 0.0) for q in range(QUARTERS)], axis=0
    )
    high = spread.astype(jnp.bfloat16)
    low = (spread - high.astype(jnp.float32)).astype(jnp.bfloat16)
    weigh_ref[...] = jnp.concatenate([high, low], axis=0)


def weigh(routes, gate_values):
    return pl.pallas_call(
        weigh_kernel,
        out_shape=jax.ShapeDtypeStruct((2 * QUARTERS * routes.shape[0], ROWS), jnp.bfloat16),
        name="slot_weights",
    )(routes, gate_values)


def combine_kernel(rows_ref, weigh_ref, out_ref, total):
    step = pl.program_id(0)
    part = jnp.dot(weigh_ref[...], rows_ref[...], preferred_element_type=jnp.float32)

    @pl.when(step == 0)
    def _():
        total[...] = part

    @pl.when(step > 0)
    def _():
        total[...] += part

    @pl.when(step == pl.num_programs(0) - 1)
    def _():
        tok_rows = out_ref.shape[0]
        half = QUARTERS * tok_rows
        width = total.shape[1]
        both = (total[:half] + total[half:]).astype(jnp.bfloat16)
        for q in range(QUARTERS):
            out_ref[:, q * width : (q + 1) * width] = both[q * tok_rows : (q + 1) * tok_rows]


def combine(returned, weights):
    width = returned.shape[1]
    tok_rows = weights.shape[0] // (2 * QUARTERS)
    return pl.pallas_call(
        combine_kernel,
        grid=(ROWS // STEP,),
        in_specs=[
            pl.BlockSpec((STEP, width), lambda j: (j, 0)),
            pl.BlockSpec((weights.shape[0], STEP), lambda j: (0, j)),
        ],
        out_specs=pl.BlockSpec((tok_rows, width * QUARTERS), lambda j: (0, 0)),
        out_shape=jax.ShapeDtypeStruct((tok_rows, width * QUARTERS), jnp.bfloat16),
        scratch_shapes=[pltpu.VMEM((weights.shape[0], width), jnp.float32)],
        compiler_params=pltpu.CompilerParams(vmem_limit_bytes=16 * 2**20),
        name="combine",
    )(returned, weights)


def attend(queries, latent_cache, lengths):
    scores = (
        jnp.einsum("rhk,rck->rhc", queries, latent_cache, preferred_element_type=jnp.float32)
        * score_scale
    )
    in_range = jnp.arange(latent_cache.shape[1])[None, None, :] < lengths[:, None, None]
    scores = jnp.where(in_range, scores, -jnp.inf)
    row_max = jnp.max(scores, axis=-1, keepdims=True)
    raised = jnp.exp(scores - row_max)
    probs = (raised / jnp.sum(raised, axis=-1, keepdims=True)).astype(jnp.bfloat16)
    attended = jnp.einsum(
        "rhc,rcl->rhl", probs, latent_cache[:, :, :LAT], preferred_element_type=jnp.float32
    )
    return attended.astype(jnp.bfloat16)


def to_other_core(rows):
    return lax.ppermute(rows, "core", [(0, 1), (1, 0)])


def between_chips(rows):
    return lax.all_to_all(rows, CHIPS, split_axis=0, concat_axis=0, tiled=True)


def shards(
    hidden, norm_gain, routes, gate_values, w_gate, w_up, w_down, queries, latent_cache, lengths
):
    far_gate, far_up, far_down = [to_other_core(w) for w in (w_gate, w_up, w_down)]
    sent = pack(hidden, norm_gain, routes)
    arrived = between_chips(sent)
    near_act = gate_up(arrived, w_gate, w_up)
    far_act = gate_up(arrived, far_gate, far_up)
    partial_rows = down(near_act, far_act, w_down, far_down)
    returned = between_chips(partial_rows)
    attn_out = attend(queries, latent_cache, lengths)
    moe_out = combine(returned, weigh(routes, gate_values))
    return (moe_out, attn_out)


def solution(mesh):
    fine = Mesh(mesh.devices.reshape(SIZES), AXES)
    placed = (
        P(AXES, None),
        P(),
        P(AXES, None),
        P(AXES, None),
        P(None, AXES),
        P(None, AXES),
        P(AXES, None),
        P(AXES, None, None),
        P(AXES, None, None),
        P(AXES),
    )
    return jax.shard_map(
        shards,
        mesh=fine,
        in_specs=placed,
        out_specs=(P(AXES, None), P(AXES, None, None)),
        check_vma=False,
    )
```

```python
import itertools

import jax
import jax.numpy as jnp
from jax import lax
from jax.experimental import pallas as pl
from jax.experimental.pallas import tpu as pltpu
from jax.sharding import Mesh, PartitionSpec as P

LAT = 512
CAP = 4

AXES = ("zl", "zh", "x", "y", "core")
SIZES = (2, 2, 4, 4, 2)
LINE = 4
STEPS = (0, 1, -1, 2)
META = 128
CHUNK = 512
LIMIT = 5

norm_eps = 1e-06
score_scale = 0.07216878364870322


def moved_along(place, axis, step):
    place = dict(place)
    if axis == "z":
        z = (place["zh"] * 2 + place["zl"] + step) % LINE
        place["zh"], place["zl"] = z // 2, z % 2
    else:
        place[axis] = (place[axis] + step) % LINE
    return place


def index_of(place):
    index = 0
    for axis, size in zip(AXES, SIZES):
        index = index * size + place[axis]
    return index


def shift(rows, axes, step):
    pairs = []
    for values in itertools.product(*[range(size) for size in SIZES]):
        place = dict(zip(AXES, values))
        pairs.append((index_of(place), index_of(moved_along(place, axes[place["core"]], step))))
    return lax.ppermute(rows, AXES, pairs)


def to_other_core(rows):
    return lax.ppermute(rows, "core", [(0, 1), (1, 0)])


def in_vmem(count):
    return [pl.BlockSpec(memory_space=pltpu.VMEM)] * count


def normalize_kernel(hidden_ref, gain_ref, routes_ref, gates_ref, out_ref):
    features = hidden_ref[...].astype(jnp.float32)
    squares = jnp.mean(features * features, axis=-1, keepdims=True)
    normed = features * lax.rsqrt(squares + norm_eps) * gain_ref[...]
    gates = gates_ref[...]
    high = gates.astype(jnp.bfloat16).astype(jnp.float32)
    tok_rows, topk = gates.shape
    rest = jnp.zeros((tok_rows, META - 3 * topk), jnp.float32)
    meta = jnp.concatenate(
        [routes_ref[...].astype(jnp.float32), high, gates - high, rest], axis=1
    )
    width = hidden_ref.shape[1]
    out_ref[:, :width] = normed.astype(jnp.bfloat16)
    out_ref[:, width:] = meta.astype(jnp.bfloat16)


def normalize(hidden, norm_gain, routes, gate_values):
    tok_rows, width = hidden.shape
    return pl.pallas_call(
        normalize_kernel,
        in_specs=in_vmem(4),
        out_specs=in_vmem(1)[0],
        out_shape=jax.ShapeDtypeStruct((tok_rows, width + META), jnp.bfloat16),
        name="normalize",
    )(hidden, norm_gain.reshape(1, -1), routes, gate_values)


def slot_table(meta, experts_ref, tok_rows, topk):
    rows = meta.shape[0]
    slots = rows // tok_rows * CAP
    shape = (rows, LINE * slots)
    row = lax.broadcasted_iota(jnp.int32, shape, 0)
    slot = lax.broadcasted_iota(jnp.int32, shape, 1)
    which = lax.broadcasted_iota(jnp.int32, (1, LINE * slots), 1) // slots
    expert = jnp.zeros(which.shape, jnp.int32)
    for n in range(LINE):
        expert = jnp.where(which == n, experts_ref[n], expert)
    expert = expert.astype(jnp.float32)
    named = jnp.zeros(shape, jnp.float32)
    high = jnp.zeros(shape, jnp.float32)
    low = jnp.zeros(shape, jnp.float32)
    for k in range(topk):
        hit = meta[:, k : k + 1] == expert
        named = jnp.where(hit, 1.0, named)
        high = jnp.where(hit, meta[:, topk + k : topk + k + 1], high)
        low = jnp.where(hit, meta[:, 2 * topk + k : 2 * topk + k + 1], low)
    to = lax.broadcasted_iota(jnp.int32, (rows, rows), 0)
    frm = lax.broadcasted_iota(jnp.int32, (rows, rows), 1)
    before = ((to // tok_rows == frm // tok_rows) & (frm < to)).astype(jnp.float32)
    rank = jnp.dot(
        before.astype(jnp.bfloat16), named.astype(jnp.bfloat16), preferred_element_type=jnp.float32
    )
    place = slot % slots
    fills = (
        (named > 0.5)
        & (row // tok_rows == place // CAP)
        & (rank == (place % CAP).astype(jnp.float32))
    )
    return fills, jnp.where(fills, high, 0.0), jnp.where(fills, low, 0.0)


def select_kernel(tok_rows, topk, experts_ref, *refs):
    pieces, outs = refs[:LINE], refs[LINE:]
    width = outs[0].shape[1]
    slots = outs[0].shape[0]
    meta = jnp.concatenate([p[:, width:] for p in pieces], axis=0).astype(jnp.float32)
    fills, _, _ = slot_table(meta, experts_ref, tok_rows, topk)
    pick = fills.astype(jnp.float32).astype(jnp.bfloat16)
    for start in range(0, width, CHUNK):
        columns = slice(start, start + CHUNK)
        rows = jnp.concatenate([p[:, columns] for p in pieces], axis=0)
        picked = lax.dot_general(
            pick, rows, (((0,), (0,)), ((), ())), preferred_element_type=jnp.float32
        ).astype(jnp.bfloat16)
        for n in range(LINE):
            outs[n][:, columns] = picked[n * slots : (n + 1) * slots]


def select(pieces, experts, tok_rows, topk):
    piece_rows = pieces[0].shape[0]
    width = pieces[0].shape[1] - META
    slots = LINE * piece_rows // tok_rows * CAP
    return pl.pallas_call(
        lambda *refs: select_kernel(tok_rows, topk, *refs),
        in_specs=[pl.BlockSpec(memory_space=pltpu.SMEM)] + in_vmem(LINE),
        out_specs=in_vmem(LINE),
        out_shape=[jax.ShapeDtypeStruct((slots, width), jnp.bfloat16)] * LINE,
        compiler_params=pltpu.CompilerParams(vmem_limit_bytes=8 * 2**20),
        cost_estimate=pl.CostEstimate(
            flops=2 * LINE * slots * LINE * piece_rows * width,
            bytes_accessed=2 * LINE * width * (slots + piece_rows),
            transcendentals=0,
        ),
        name="select_slots",
    )(experts, *pieces)


def weigh_kernel(tok_rows, topk, experts_ref, *refs):
    metas, weigh_ref = refs[:LINE], refs[LINE]
    meta = jnp.concatenate([m[:, -META:] for m in metas], axis=0).astype(jnp.float32)
    _, high, low = slot_table(meta, experts_ref, tok_rows, topk)
    weigh_ref[...] = jnp.concatenate([high, low], axis=0).astype(jnp.bfloat16)


def weigh(pieces, experts, tok_rows, topk):
    piece_rows = pieces[0].shape[0]
    rows = LINE * piece_rows
    slots = rows // tok_rows * CAP
    return pl.pallas_call(
        lambda *refs: weigh_kernel(tok_rows, topk, *refs),
        in_specs=[pl.BlockSpec(memory_space=pltpu.SMEM)] + in_vmem(LINE),
        out_specs=in_vmem(1)[0],
        out_shape=jax.ShapeDtypeStruct((2 * rows, LINE * slots), jnp.bfloat16),
        name="slot_weights",
    )(experts, *pieces)


def load_kernel(count, *refs):
    stored, loaded, arrived = refs[:count], refs[count : 2 * count], refs[2 * count]
    fetches = [
        pltpu.make_async_copy(source, target, arrived.at[n])
        for n, (source, target) in enumerate(zip(stored, loaded))
    ]
    for fetch in fetches:
        fetch.start()
    for fetch in fetches:
        fetch.wait()


def load(weights):
    count = len(weights)
    return pl.pallas_call(
        lambda *refs: load_kernel(count, *refs),
        in_specs=[pl.BlockSpec(memory_space=pltpu.HBM)] * count,
        out_specs=in_vmem(count),
        out_shape=[jax.ShapeDtypeStruct(w.shape, jnp.bfloat16) for w in weights],
        scratch_shapes=[pltpu.SemaphoreType.DMA((count,))],
        compiler_params=pltpu.CompilerParams(vmem_limit_bytes=LIMIT * 2**20),
        cost_estimate=pl.CostEstimate(
            flops=0, bytes_accessed=2 * sum(w.size for w in weights), transcendentals=0
        ),
        name="load_weights",
    )(*weights)


def experts_kernel(count, *refs):
    pieces, refs = refs[:count], refs[count:]
    near, far, outs = refs[:3], refs[3:6], refs[6:]
    rows = jnp.concatenate([piece[...] for piece in pieces], axis=0)
    piece_rows, width = pieces[0].shape

    def activate(gates, ups):
        gate = jnp.dot(rows, gates[...], preferred_element_type=jnp.float32)
        up = jnp.dot(rows, ups[...], preferred_element_type=jnp.float32)
        return (gate / (1.0 + jnp.exp(-gate)) * up).astype(jnp.bfloat16)

    near_act = activate(near[0], near[1])
    far_act = activate(far[0], far[1])
    for start in range(0, width, CHUNK):
        columns = slice(start, start + CHUNK)
        total = (
            jnp.dot(near_act, near[2][:, columns], preferred_element_type=jnp.float32)
            + jnp.dot(far_act, far[2][:, columns], preferred_element_type=jnp.float32)
        ).astype(jnp.bfloat16)
        for n, out in enumerate(outs):
            out[:, columns] = total[n * piece_rows : (n + 1) * piece_rows]


def run_experts(pieces, near, far):
    count = len(pieces)
    piece_rows, width = pieces[0].shape
    size = sum(w.size for w in near) + sum(w.size for w in far)
    return pl.pallas_call(
        lambda *refs: experts_kernel(count, *refs),
        in_specs=in_vmem(count + 6),
        out_specs=in_vmem(count),
        out_shape=[jax.ShapeDtypeStruct((piece_rows, width), jnp.bfloat16)] * count,
        compiler_params=pltpu.CompilerParams(vmem_limit_bytes=LIMIT * 2**20),
        cost_estimate=pl.CostEstimate(
            flops=2 * count * piece_rows * size, bytes_accessed=2 * size, transcendentals=0
        ),
        name="experts",
    )(*pieces, *near, *far)


def spread_kernel(weigh_ref, *refs):
    pieces, outs = refs[:LINE], refs[LINE:]
    count, width = outs[0].shape
    half = weigh_ref.shape[0] // 2
    for start in range(0, width, CHUNK):
        columns = slice(start, start + CHUNK)
        rows = jnp.concatenate([p[:, columns] for p in pieces], axis=0)
        both = jnp.dot(weigh_ref[...], rows, preferred_element_type=jnp.float32)
        total = (both[:half] + both[half:]).astype(jnp.bfloat16)
        for n in range(LINE):
            outs[n][:, columns] = total[n * count : (n + 1) * count]


def spread(weights, pieces):
    slots, width = pieces[0].shape
    rows = weights.shape[0] // 2
    return pl.pallas_call(
        spread_kernel,
        in_specs=in_vmem(1 + LINE),
        out_specs=in_vmem(LINE),
        out_shape=[jax.ShapeDtypeStruct((rows // LINE, width), jnp.bfloat16)] * LINE,
        compiler_params=pltpu.CompilerParams(vmem_limit_bytes=8 * 2**20),
        cost_estimate=pl.CostEstimate(
            flops=2 * 2 * rows * LINE * slots * width,
            bytes_accessed=2 * width * (LINE * slots + rows),
            transcendentals=0,
        ),
        name="spread_slots",
    )(weights, *pieces)


def add_kernel(parts, *refs):
    pieces, outs = refs[:LINE], refs[LINE:]
    total = pieces[0][...].astype(jnp.float32)
    for piece in pieces[1:]:
        total = total + piece[...].astype(jnp.float32)
    count = outs[0].shape[0]
    for n in range(parts):
        outs[n][...] = total[n * count : (n + 1) * count].astype(jnp.bfloat16)


def add(pieces, parts):
    rows, width = pieces[0].shape
    return pl.pallas_call(
        lambda *refs: add_kernel(parts, *refs),
        in_specs=in_vmem(LINE),
        out_specs=in_vmem(parts),
        out_shape=[jax.ShapeDtypeStruct((rows // parts, width), jnp.bfloat16)] * parts,
        compiler_params=pltpu.CompilerParams(vmem_limit_bytes=8 * 2**20),
        cost_estimate=pl.CostEstimate(
            flops=LINE * rows * width,
            bytes_accessed=2 * (LINE + 1) * rows * width,
            transcendentals=0,
        ),
        name="add_pieces",
    )(*pieces)


def attend(queries, latent_cache, lengths):
    scores = (
        jnp.einsum("rhk,rck->rhc", queries, latent_cache, preferred_element_type=jnp.float32)
        * score_scale
    )
    in_range = jnp.arange(latent_cache.shape[1])[None, None, :] < lengths[:, None, None]
    scores = jnp.where(in_range, scores, -jnp.inf)
    row_max = jnp.max(scores, axis=-1, keepdims=True)
    raised = jnp.exp(scores - row_max)
    probs = (raised / jnp.sum(raised, axis=-1, keepdims=True)).astype(jnp.bfloat16)
    attended = jnp.einsum(
        "rhc,rcl->rhl", probs, latent_cache[:, :, :LAT], preferred_element_type=jnp.float32
    )
    return attended.astype(jnp.bfloat16)


FIRST = ("y", "y")
SECOND = ("x", "z")
THIRD = ("z", "x")


def target_experts():
    zl, zh, x, y, core = [lax.axis_index(axis) for axis in AXES]
    z = zh * 2 + zl
    found = []
    for step in STEPS:
        to_z = jnp.where(core == 0, (z + step) % LINE, z)
        to_x = jnp.where(core == 0, x, (x + step) % LINE)
        found.append((((to_z % 2) * 2 + to_z // 2) * 4 + to_x) * 2 + y // 2)
    return jnp.stack(found).astype(jnp.int32)


def gather_line(rows, axes):
    return [rows] + [shift(rows, axes, step) for step in STEPS[1:]]


def hand_out(pieces, axes):
    return [pieces[0]] + [shift(p, axes, step) for p, step in zip(pieces[1:], STEPS[1:])]


def hand_back(piece, axes, step):
    return shift(piece, axes, -step)


def shards(
    hidden, norm_gain, routes, gate_values, w_gate, w_up, w_down, queries, latent_cache, lengths
):
    tok_rows, topk = routes.shape
    experts = target_experts()
    far_gate = to_other_core(w_gate)
    own = normalize(hidden, norm_gain, routes, gate_values)
    line = jnp.concatenate(gather_line(own, FIRST), axis=0)
    line, w_up = lax.optimization_barrier((line, w_up))
    far_up = to_other_core(w_up)
    plane = gather_line(line, SECOND)
    plane, w_gate, w_up, w_down, far_gate = lax.optimization_barrier(
        (plane, w_gate, w_up, w_down, far_gate)
    )
    far_down = to_other_core(w_down)
    slots = hand_out(select(plane, experts, tok_rows, topk), THIRD)
    weights = weigh(plane, experts, tok_rows, topk)
    attn_out = attend(queries, latent_cache, lengths)

    loaded = load((w_gate, w_up, w_down, far_gate, far_up, far_down))
    results = []
    for group in (slots[:2], slots[2:]):
        group, loaded, results = lax.optimization_barrier((group, loaded, results))
        results = results + list(run_experts(group, loaded[:3], loaded[3:]))
    back = [results[0]] + [
        hand_back(piece, THIRD, step) for piece, step in zip(results[1:], STEPS[1:])
    ]
    dense = spread(weights, back)
    dense = [dense[0]] + [
        hand_back(piece, SECOND, step) for piece, step in zip(dense[1:], STEPS[1:])
    ]
    sums = add(dense, LINE)
    sums = [sums[0]] + [hand_back(piece, FIRST, step) for piece, step in zip(sums[1:], STEPS[1:])]
    (moe_out,) = add(sums, 1)
    return (moe_out, attn_out)


def solution(mesh):
    fine = Mesh(mesh.devices.reshape(SIZES), AXES)
    placed = (
        P(AXES, None),
        P(),
        P(AXES, None),
        P(AXES, None),
        P(None, AXES),
        P(None, AXES),
        P(AXES, None),
        P(AXES, None, None),
        P(AXES, None, None),
        P(AXES),
    )
    return jax.shard_map(
        shards,
        mesh=fine,
        in_specs=placed,
        out_specs=(P(AXES, None), P(AXES, None, None)),
        check_vma=False,
    )
```

```python
import itertools

import jax
import jax.numpy as jnp
from jax import lax
from jax.experimental import pallas as pl
from jax.experimental.pallas import tpu as pltpu
from jax.sharding import Mesh, PartitionSpec as P

LAT = 512
CAP = 4

AXES = ("zl", "zh", "x", "y", "core")
SIZES = (2, 2, 4, 4, 2)
LINE = 4
STEPS = (0, 2, 1, -1)
EARLY = 2
META = 128
CHUNK = 512
LIMIT = 5

norm_eps = 1e-06
score_scale = 0.07216878364870322


def moved_along(place, axis, step):
    place = dict(place)
    if axis == "z":
        z = (place["zh"] * 2 + place["zl"] + step) % LINE
        place["zh"], place["zl"] = z // 2, z % 2
    else:
        place[axis] = (place[axis] + step) % LINE
    return place


def index_of(place):
    index = 0
    for axis, size in zip(AXES, SIZES):
        index = index * size + place[axis]
    return index


def shift(rows, axes, step):
    pairs = []
    for values in itertools.product(*[range(size) for size in SIZES]):
        place = dict(zip(AXES, values))
        pairs.append((index_of(place), index_of(moved_along(place, axes[place["core"]], step))))
    return lax.ppermute(rows, AXES, pairs)


def to_other_core(rows):
    return lax.ppermute(rows, "core", [(0, 1), (1, 0)])


def in_vmem(count):
    return [pl.BlockSpec(memory_space=pltpu.VMEM)] * count


def normalize_kernel(hidden_ref, gain_ref, routes_ref, gates_ref, out_ref):
    features = hidden_ref[...].astype(jnp.float32)
    squares = jnp.mean(features * features, axis=-1, keepdims=True)
    normed = features * lax.rsqrt(squares + norm_eps) * gain_ref[...]
    gates = gates_ref[...]
    high = gates.astype(jnp.bfloat16).astype(jnp.float32)
    tok_rows, topk = gates.shape
    rest = jnp.zeros((tok_rows, META - 3 * topk), jnp.float32)
    meta = jnp.concatenate(
        [routes_ref[...].astype(jnp.float32), high, gates - high, rest], axis=1
    )
    width = hidden_ref.shape[1]
    out_ref[:, :width] = normed.astype(jnp.bfloat16)
    out_ref[:, width:] = meta.astype(jnp.bfloat16)


def normalize(hidden, norm_gain, routes, gate_values):
    tok_rows, width = hidden.shape
    return pl.pallas_call(
        normalize_kernel,
        in_specs=in_vmem(4),
        out_specs=in_vmem(1)[0],
        out_shape=jax.ShapeDtypeStruct((tok_rows, width + META), jnp.bfloat16),
        compiler_params=pltpu.CompilerParams(vmem_limit_bytes=LIMIT * 2**20),
        name="normalize",
    )(hidden, norm_gain.reshape(1, -1), routes, gate_values)


def slot_table(meta, experts_ref, tok_rows, topk):
    rows = meta.shape[0]
    slots = rows // tok_rows * CAP
    shape = (rows, LINE * slots)
    row = lax.broadcasted_iota(jnp.int32, shape, 0)
    slot = lax.broadcasted_iota(jnp.int32, shape, 1)
    which = lax.broadcasted_iota(jnp.int32, (1, LINE * slots), 1) // slots
    expert = jnp.zeros(which.shape, jnp.int32)
    for n in range(LINE):
        expert = jnp.where(which == n, experts_ref[n], expert)
    expert = expert.astype(jnp.float32)
    named = jnp.zeros(shape, jnp.float32)
    high = jnp.zeros(shape, jnp.float32)
    low = jnp.zeros(shape, jnp.float32)
    for k in range(topk):
        hit = meta[:, k : k + 1] == expert
        named = jnp.where(hit, 1.0, named)
        high = jnp.where(hit, meta[:, topk + k : topk + k + 1], high)
        low = jnp.where(hit, meta[:, 2 * topk + k : 2 * topk + k + 1], low)
    to = lax.broadcasted_iota(jnp.int32, (rows, rows), 0)
    frm = lax.broadcasted_iota(jnp.int32, (rows, rows), 1)
    before = ((to // tok_rows == frm // tok_rows) & (frm < to)).astype(jnp.float32)
    rank = jnp.dot(
        before.astype(jnp.bfloat16), named.astype(jnp.bfloat16), preferred_element_type=jnp.float32
    )
    place = slot % slots
    fills = (
        (named > 0.5)
        & (row // tok_rows == place // CAP)
        & (rank == (place % CAP).astype(jnp.float32))
    )
    return fills, jnp.where(fills, high, 0.0), jnp.where(fills, low, 0.0)


def select_kernel(tok_rows, topk, experts_ref, *refs):
    pieces, outs = refs[:LINE], refs[LINE:]
    width = outs[0].shape[1]
    slots = outs[0].shape[0]
    meta = jnp.concatenate([p[:, width:] for p in pieces], axis=0).astype(jnp.float32)
    fills, _, _ = slot_table(meta, experts_ref, tok_rows, topk)
    pick = fills.astype(jnp.float32).astype(jnp.bfloat16)
    for start in range(0, width, CHUNK):
        columns = slice(start, start + CHUNK)
        rows = jnp.concatenate([p[:, columns] for p in pieces], axis=0)
        picked = lax.dot_general(
            pick, rows, (((0,), (0,)), ((), ())), preferred_element_type=jnp.float32
        ).astype(jnp.bfloat16)
        for n in range(LINE):
            outs[n][:, columns] = picked[n * slots : (n + 1) * slots]


def select(pieces, experts, tok_rows, topk):
    piece_rows = pieces[0].shape[0]
    width = pieces[0].shape[1] - META
    slots = LINE * piece_rows // tok_rows * CAP
    return pl.pallas_call(
        lambda *refs: select_kernel(tok_rows, topk, *refs),
        in_specs=[pl.BlockSpec(memory_space=pltpu.SMEM)] + in_vmem(LINE),
        out_specs=in_vmem(LINE),
        out_shape=[jax.ShapeDtypeStruct((slots, width), jnp.bfloat16)] * LINE,
        compiler_params=pltpu.CompilerParams(vmem_limit_bytes=LIMIT * 2**20),
        cost_estimate=pl.CostEstimate(
            flops=2 * LINE * slots * LINE * piece_rows * width,
            bytes_accessed=2 * LINE * width * (slots + piece_rows),
            transcendentals=0,
        ),
        name="select_slots",
    )(experts, *pieces)


def weigh_kernel(tok_rows, topk, experts_ref, *refs):
    metas, weigh_ref = refs[:LINE], refs[LINE]
    meta = jnp.concatenate([m[:, -META:] for m in metas], axis=0).astype(jnp.float32)
    _, high, low = slot_table(meta, experts_ref, tok_rows, topk)
    weigh_ref[...] = jnp.concatenate([high, low], axis=0).astype(jnp.bfloat16)


def weigh(pieces, experts, tok_rows, topk):
    piece_rows = pieces[0].shape[0]
    rows = LINE * piece_rows
    slots = rows // tok_rows * CAP
    return pl.pallas_call(
        lambda *refs: weigh_kernel(tok_rows, topk, *refs),
        in_specs=[pl.BlockSpec(memory_space=pltpu.SMEM)] + in_vmem(LINE),
        out_specs=in_vmem(1)[0],
        out_shape=jax.ShapeDtypeStruct((2 * rows, LINE * slots), jnp.bfloat16),
        compiler_params=pltpu.CompilerParams(vmem_limit_bytes=LIMIT * 2**20),
        name="slot_weights",
    )(experts, *pieces)


def load_kernel(count, *refs):
    stored, loaded, arrived = refs[:count], refs[count : 2 * count], refs[-1]
    fetches = [
        pltpu.make_async_copy(source, target, arrived.at[n])
        for n, (source, target) in enumerate(zip(stored, loaded))
    ]
    for fetch in fetches:
        fetch.start()
    for fetch in fetches:
        fetch.wait()


def load(weights, room):
    count = len(weights)
    shapes = [w.shape for w in weights] + [room]
    return pl.pallas_call(
        lambda *refs: load_kernel(count, *refs),
        in_specs=[pl.BlockSpec(memory_space=pltpu.HBM)] * count,
        out_specs=in_vmem(count + 1),
        out_shape=[jax.ShapeDtypeStruct(shape, jnp.bfloat16) for shape in shapes],
        scratch_shapes=[pltpu.SemaphoreType.DMA((count,))],
        compiler_params=pltpu.CompilerParams(vmem_limit_bytes=LIMIT * 2**20),
        cost_estimate=pl.CostEstimate(
            flops=600 * sum(w.size for w in weights), bytes_accessed=0, transcendentals=0
        ),
        name="load_weights",
    )(*weights)


def apply_experts(pieces, near, far, down_ready, outs):
    rows = jnp.concatenate([piece[...] for piece in pieces], axis=0)
    piece_rows, width = pieces[0].shape

    def activate(gates, ups):
        gate = jnp.dot(rows, gates[...], preferred_element_type=jnp.float32)
        up = jnp.dot(rows, ups[...], preferred_element_type=jnp.float32)
        return (gate / (1.0 + jnp.exp(-gate)) * up).astype(jnp.bfloat16)

    near_act = activate(near[0], near[1])
    far_act = activate(far[0], far[1])
    down_ready()
    for start in range(0, width, CHUNK):
        columns = slice(start, start + CHUNK)
        total = (
            jnp.dot(near_act, near[2][:, columns], preferred_element_type=jnp.float32)
            + jnp.dot(far_act, far[2][:, columns], preferred_element_type=jnp.float32)
        ).astype(jnp.bfloat16)
        for n, out in enumerate(outs):
            out[:, columns] = total[n * piece_rows : (n + 1) * piece_rows]


def first_kernel(count, *refs):
    pieces, weights, stored = refs[:count], refs[count : count + 5], refs[count + 6]
    outs, loaded, arrived = refs[count + 7 : -2], refs[-2], refs[-1]
    fetch = pltpu.make_async_copy(stored, loaded, arrived)
    fetch.start()
    apply_experts(pieces, weights[:3], list(weights[3:]) + [loaded], fetch.wait, outs)


def later_kernel(count, *refs):
    pieces, weights, outs = refs[:count], refs[count : count + 6], refs[count + 6 :]
    apply_experts(pieces, weights[:3], weights[3:], lambda: None, outs)


def run_experts(pieces, weights, stored=None):
    count = len(pieces)
    piece_rows, width = pieces[0].shape
    results = [jax.ShapeDtypeStruct((piece_rows, width), jnp.bfloat16)] * count
    in_specs = in_vmem(count + len(weights))
    operands = [*pieces, *weights]
    scratch = []
    aliases = {}
    kernel = later_kernel
    if stored is not None:
        kernel = first_kernel
        in_specs.append(pl.BlockSpec(memory_space=pltpu.HBM))
        operands.append(stored)
        aliases = {len(operands) - 2: len(results)}
        results.append(jax.ShapeDtypeStruct(stored.shape, stored.dtype))
        scratch.append(pltpu.SemaphoreType.DMA)
    size = sum(w.size for w in weights)
    return pl.pallas_call(
        lambda *refs: kernel(count, *refs),
        in_specs=in_specs,
        out_specs=in_vmem(len(results)),
        out_shape=results,
        scratch_shapes=scratch,
        input_output_aliases=aliases,
        compiler_params=pltpu.CompilerParams(vmem_limit_bytes=LIMIT * 2**20),
        cost_estimate=pl.CostEstimate(
            flops=2 * count * piece_rows * size, bytes_accessed=2 * size, transcendentals=0
        ),
        name="experts",
    )(*operands)


def spread_kernel(first_slot, count, *refs):
    weigh_ref, pieces, refs = refs[0], refs[1 : 1 + count], refs[1 + count :]
    half = weigh_ref.shape[0] // 2
    piece_rows, width = pieces[0].shape
    slots = slice(first_slot, first_slot + count * piece_rows)
    outs = refs if first_slot == 0 else refs[1:]
    for start in range(0, width, CHUNK):
        columns = slice(start, start + CHUNK)
        rows = jnp.concatenate([p[:, columns] for p in pieces], axis=0)
        both = jnp.dot(weigh_ref[:, slots], rows, preferred_element_type=jnp.float32)
        total = both[:half] + both[half:]
        if first_slot > 0:
            total = (total + refs[0][:, columns]).astype(jnp.bfloat16)
        for n, out in enumerate(outs):
            out[:, columns] = total[n * out.shape[0] : (n + 1) * out.shape[0]]


def spread(weights, pieces, begun=None):
    slots, width = pieces[0].shape
    rows = weights.shape[0] // 2
    first_slot = 0 if begun is None else EARLY * slots
    results = [jax.ShapeDtypeStruct((rows, width), jnp.float32)]
    operands = [weights, *pieces]
    if begun is not None:
        results = [jax.ShapeDtypeStruct((rows // LINE, width), jnp.bfloat16)] * LINE
        operands.append(begun)
    return pl.pallas_call(
        lambda *refs: spread_kernel(first_slot, len(pieces), *refs),
        in_specs=in_vmem(len(operands)),
        out_specs=in_vmem(len(results)),
        out_shape=results,
        compiler_params=pltpu.CompilerParams(vmem_limit_bytes=LIMIT * 2**20),
        cost_estimate=pl.CostEstimate(
            flops=2 * 2 * rows * len(pieces) * slots * width,
            bytes_accessed=2 * width * (len(pieces) * slots + 2 * rows),
            transcendentals=0,
        ),
        name="spread_slots",
    )(*operands)


def add_kernel(parts, *refs):
    pieces, outs = refs[:LINE], refs[LINE:]
    total = pieces[0][...].astype(jnp.float32)
    for piece in pieces[1:]:
        total = total + piece[...].astype(jnp.float32)
    count = outs[0].shape[0]
    for n in range(parts):
        outs[n][...] = total[n * count : (n + 1) * count].astype(jnp.bfloat16)


def add(pieces, parts):
    rows, width = pieces[0].shape
    return pl.pallas_call(
        lambda *refs: add_kernel(parts, *refs),
        in_specs=in_vmem(LINE),
        out_specs=in_vmem(parts),
        out_shape=[jax.ShapeDtypeStruct((rows // parts, width), jnp.bfloat16)] * parts,
        compiler_params=pltpu.CompilerParams(vmem_limit_bytes=LIMIT * 2**20),
        cost_estimate=pl.CostEstimate(
            flops=LINE * rows * width,
            bytes_accessed=2 * (LINE + 1) * rows * width,
            transcendentals=0,
        ),
        name="add_pieces",
    )(*pieces)


def attend(queries, latent_cache, lengths):
    scores = (
        jnp.einsum("rhk,rck->rhc", queries, latent_cache, preferred_element_type=jnp.float32)
        * score_scale
    )
    in_range = jnp.arange(latent_cache.shape[1])[None, None, :] < lengths[:, None, None]
    scores = jnp.where(in_range, scores, -jnp.inf)
    row_max = jnp.max(scores, axis=-1, keepdims=True)
    raised = jnp.exp(scores - row_max)
    probs = (raised / jnp.sum(raised, axis=-1, keepdims=True)).astype(jnp.bfloat16)
    attended = jnp.einsum(
        "rhc,rcl->rhl", probs, latent_cache[:, :, :LAT], preferred_element_type=jnp.float32
    )
    return attended.astype(jnp.bfloat16)


FIRST = ("y", "y")
SECOND = ("x", "z")
THIRD = ("z", "x")


def target_experts():
    zl, zh, x, y, core = [lax.axis_index(axis) for axis in AXES]
    z = zh * 2 + zl
    found = []
    for step in STEPS:
        to_z = jnp.where(core == 0, (z + step) % LINE, z)
        to_x = jnp.where(core == 0, x, (x + step) % LINE)
        found.append((((to_z % 2) * 2 + to_z // 2) * 4 + to_x) * 2 + y // 2)
    return jnp.stack(found).astype(jnp.int32)


def gather_line(rows, axes):
    return [rows] + [shift(rows, axes, step) for step in STEPS[1:]]


def hand_out(pieces, axes):
    return [pieces[0]] + [shift(p, axes, step) for p, step in zip(pieces[1:], STEPS[1:])]


def hand_back(piece, axes, step):
    return shift(piece, axes, -step)


def shards(
    hidden, norm_gain, routes, gate_values, w_gate, w_up, w_down, queries, latent_cache, lengths
):
    tok_rows, topk = routes.shape
    experts = target_experts()
    far_gate = to_other_core(w_gate)
    own = normalize(hidden, norm_gain, routes, gate_values)
    line = jnp.concatenate(gather_line(own, FIRST), axis=0)
    line, w_up = lax.optimization_barrier((line, w_up))
    far_up = to_other_core(w_up)
    plane = gather_line(line, SECOND)
    plane, w_gate, w_up, w_down, far_gate = lax.optimization_barrier(
        (plane, w_gate, w_up, w_down, far_gate)
    )
    far_down = to_other_core(w_down)
    slots = hand_out(select(plane, experts, tok_rows, topk), THIRD)
    weights = weigh(plane, experts, tok_rows, topk)
    attn_out = attend(queries, latent_cache, lengths)

    loaded = load((w_gate, w_up, w_down, far_gate, far_up), w_down.shape)
    group, loaded = lax.optimization_barrier((slots[:EARLY], loaded))
    *results, last = run_experts(group, loaded, far_down)
    group, loaded, last = lax.optimization_barrier((slots[EARLY:], loaded[:5], last))
    results = results + list(run_experts(group, [*loaded, last]))
    back = [results[0]] + [
        hand_back(piece, THIRD, step) for piece, step in zip(results[1:], STEPS[1:])
    ]
    (begun,) = spread(weights, back[:EARLY])
    begun, late = lax.optimization_barrier((begun, back[EARLY:]))
    dense = spread(weights, late, begun)
    dense = [dense[0]] + [
        hand_back(piece, SECOND, step) for piece, step in zip(dense[1:], STEPS[1:])
    ]
    sums = add(dense, LINE)
    sums = [sums[0]] + [hand_back(piece, FIRST, step) for piece, step in zip(sums[1:], STEPS[1:])]
    (moe_out,) = add(sums, 1)
    return (moe_out, attn_out)


def solution(mesh):
    fine = Mesh(mesh.devices.reshape(SIZES), AXES)
    placed = (
        P(AXES, None),
        P(),
        P(AXES, None),
        P(AXES, None),
        P(None, AXES),
        P(None, AXES),
        P(AXES, None),
        P(AXES, None, None),
        P(AXES, None, None),
        P(AXES),
    )
    return jax.shard_map(
        shards,
        mesh=fine,
        in_specs=placed,
        out_specs=(P(AXES, None), P(AXES, None, None)),
        check_vma=False,
    )
```

```python
import itertools

import jax
import jax.numpy as jnp
from jax import lax
from jax.experimental import pallas as pl
from jax.experimental.pallas import tpu as pltpu
from jax.sharding import Mesh, PartitionSpec as P

LAT = 512
CAP = 4

AXES = ("zl", "zh", "x", "y", "core")
SIZES = (2, 2, 4, 4, 2)
LINE = 4
STEPS = (0, 2, 1, -1)
EARLY = 2
META = 128
CHUNK = 512
LIMIT = 5

norm_eps = 1e-06
score_scale = 0.07216878364870322


def moved_along(place, axis, step):
    place = dict(place)
    if axis == "z":
        z = (place["zh"] * 2 + place["zl"] + step) % LINE
        place["zh"], place["zl"] = z // 2, z % 2
    else:
        place[axis] = (place[axis] + step) % LINE
    return place


def index_of(place):
    index = 0
    for axis, size in zip(AXES, SIZES):
        index = index * size + place[axis]
    return index


def shift(rows, axes, step):
    pairs = []
    for values in itertools.product(*[range(size) for size in SIZES]):
        place = dict(zip(AXES, values))
        pairs.append((index_of(place), index_of(moved_along(place, axes[place["core"]], step))))
    return lax.ppermute(rows, AXES, pairs)


def to_other_core(rows):
    return lax.ppermute(rows, "core", [(0, 1), (1, 0)])


def in_vmem(count):
    return [pl.BlockSpec(memory_space=pltpu.VMEM)] * count


def normalize_kernel(*refs):
    stored, out_ref, held, arrived = refs[:4], refs[4], refs[5:9], refs[9]
    fetches = [
        pltpu.make_async_copy(source, target, arrived.at[n])
        for n, (source, target) in enumerate(zip(stored, held))
    ]
    for fetch in fetches:
        fetch.start()
    for fetch in fetches:
        fetch.wait()
    hidden_ref, gain_ref, routes_ref, gates_ref = held
    features = hidden_ref[...].astype(jnp.float32)
    squares = jnp.mean(features * features, axis=-1, keepdims=True)
    normed = features * lax.rsqrt(squares + norm_eps) * gain_ref[...]
    gates = gates_ref[...]
    high = gates.astype(jnp.bfloat16).astype(jnp.float32)
    tok_rows, topk = gates.shape
    rest = jnp.zeros((tok_rows, META - 3 * topk), jnp.float32)
    meta = jnp.concatenate(
        [routes_ref[...].astype(jnp.float32), high, gates - high, rest], axis=1
    )
    width = hidden_ref.shape[1]
    out_ref[:, :width] = normed.astype(jnp.bfloat16)
    out_ref[:, width:] = meta.astype(jnp.bfloat16)


def normalize(hidden, norm_gain, routes, gate_values):
    tok_rows, width = hidden.shape
    operands = (hidden, norm_gain.reshape(1, -1), routes, gate_values)
    return pl.pallas_call(
        normalize_kernel,
        in_specs=[pl.BlockSpec(memory_space=pltpu.HBM)] * 4,
        out_specs=in_vmem(1)[0],
        out_shape=jax.ShapeDtypeStruct((tok_rows, width + META), jnp.bfloat16),
        scratch_shapes=[pltpu.VMEM(operand.shape, operand.dtype) for operand in operands]
        + [pltpu.SemaphoreType.DMA((4,))],
        name="normalize",
    )(*operands)


def slot_table(meta, experts_ref, tok_rows, topk):
    rows = meta.shape[0]
    slots = rows // tok_rows * CAP
    shape = (rows, LINE * slots)
    row = lax.broadcasted_iota(jnp.int32, shape, 0)
    slot = lax.broadcasted_iota(jnp.int32, shape, 1)
    which = lax.broadcasted_iota(jnp.int32, (1, LINE * slots), 1) // slots
    expert = jnp.zeros(which.shape, jnp.int32)
    for n in range(LINE):
        expert = jnp.where(which == n, experts_ref[n], expert)
    expert = expert.astype(jnp.float32)
    named = jnp.zeros(shape, jnp.float32)
    high = jnp.zeros(shape, jnp.float32)
    low = jnp.zeros(shape, jnp.float32)
    for k in range(topk):
        hit = meta[:, k : k + 1] == expert
        named = jnp.where(hit, 1.0, named)
        high = jnp.where(hit, meta[:, topk + k : topk + k + 1], high)
        low = jnp.where(hit, meta[:, 2 * topk + k : 2 * topk + k + 1], low)
    to = lax.broadcasted_iota(jnp.int32, (rows, rows), 0)
    frm = lax.broadcasted_iota(jnp.int32, (rows, rows), 1)
    before = ((to // tok_rows == frm // tok_rows) & (frm < to)).astype(jnp.float32)
    rank = jnp.dot(
        before.astype(jnp.bfloat16), named.astype(jnp.bfloat16), preferred_element_type=jnp.float32
    )
    place = slot % slots
    fills = (
        (named > 0.5)
        & (row // tok_rows == place // CAP)
        & (rank == (place % CAP).astype(jnp.float32))
    )
    return fills, jnp.where(fills, high, 0.0), jnp.where(fills, low, 0.0)


def select_kernel(tok_rows, topk, experts_ref, *refs):
    pieces, outs = refs[:LINE], refs[LINE:]
    width = outs[0].shape[1]
    slots = outs[0].shape[0]
    meta = jnp.concatenate([p[:, width:] for p in pieces], axis=0).astype(jnp.float32)
    fills, _, _ = slot_table(meta, experts_ref, tok_rows, topk)
    pick = fills.astype(jnp.float32).astype(jnp.bfloat16)
    for start in range(0, width, CHUNK):
        columns = slice(start, start + CHUNK)
        rows = jnp.concatenate([p[:, columns] for p in pieces], axis=0)
        picked = lax.dot_general(
            pick, rows, (((0,), (0,)), ((), ())), preferred_element_type=jnp.float32
        ).astype(jnp.bfloat16)
        for n in range(LINE):
            outs[n][:, columns] = picked[n * slots : (n + 1) * slots]


def select(pieces, experts, tok_rows, topk):
    piece_rows = pieces[0].shape[0]
    width = pieces[0].shape[1] - META
    slots = LINE * piece_rows // tok_rows * CAP
    return pl.pallas_call(
        lambda *refs: select_kernel(tok_rows, topk, *refs),
        in_specs=[pl.BlockSpec(memory_space=pltpu.SMEM)] + in_vmem(LINE),
        out_specs=in_vmem(LINE),
        out_shape=[jax.ShapeDtypeStruct((slots, width), jnp.bfloat16)] * LINE,
        compiler_params=pltpu.CompilerParams(vmem_limit_bytes=LIMIT * 2**20),
        cost_estimate=pl.CostEstimate(
            flops=2 * LINE * slots * LINE * piece_rows * width,
            bytes_accessed=2 * LINE * width * (slots + piece_rows),
            transcendentals=0,
        ),
        name="select_slots",
    )(experts, *pieces)


def weigh_kernel(tok_rows, topk, experts_ref, *refs):
    metas, weigh_ref = refs[:LINE], refs[LINE]
    meta = jnp.concatenate([m[:, -META:] for m in metas], axis=0).astype(jnp.float32)
    _, high, low = slot_table(meta, experts_ref, tok_rows, topk)
    weigh_ref[...] = jnp.concatenate([high, low], axis=0).astype(jnp.bfloat16)


def weigh(pieces, experts, tok_rows, topk):
    piece_rows = pieces[0].shape[0]
    rows = LINE * piece_rows
    slots = rows // tok_rows * CAP
    return pl.pallas_call(
        lambda *refs: weigh_kernel(tok_rows, topk, *refs),
        in_specs=[pl.BlockSpec(memory_space=pltpu.SMEM)] + in_vmem(LINE),
        out_specs=in_vmem(1)[0],
        out_shape=jax.ShapeDtypeStruct((2 * rows, LINE * slots), jnp.bfloat16),
        compiler_params=pltpu.CompilerParams(vmem_limit_bytes=LIMIT * 2**20),
        name="slot_weights",
    )(experts, *pieces)


def load_kernel(count, *refs):
    stored, loaded, arrived = refs[:count], refs[count : 2 * count], refs[-1]
    fetches = [
        pltpu.make_async_copy(source, target, arrived.at[n])
        for n, (source, target) in enumerate(zip(stored, loaded))
    ]
    for fetch in fetches:
        fetch.start()
    for fetch in fetches:
        fetch.wait()


def load(weights, room):
    count = len(weights)
    shapes = [w.shape for w in weights] + [room]
    return pl.pallas_call(
        lambda *refs: load_kernel(count, *refs),
        in_specs=[pl.BlockSpec(memory_space=pltpu.HBM)] * count,
        out_specs=in_vmem(count + 1),
        out_shape=[jax.ShapeDtypeStruct(shape, jnp.bfloat16) for shape in shapes],
        scratch_shapes=[pltpu.SemaphoreType.DMA((count,))],
        compiler_params=pltpu.CompilerParams(vmem_limit_bytes=LIMIT * 2**20),
        cost_estimate=pl.CostEstimate(
            flops=600 * sum(w.size for w in weights), bytes_accessed=0, transcendentals=0
        ),
        name="load_weights",
    )(*weights)


def apply_experts(pieces, near, far, down_ready, outs):
    rows = jnp.concatenate([piece[...] for piece in pieces], axis=0)
    piece_rows, width = pieces[0].shape

    def activate(gates, ups):
        gate = jnp.dot(rows, gates[...], preferred_element_type=jnp.float32)
        up = jnp.dot(rows, ups[...], preferred_element_type=jnp.float32)
        return (gate / (1.0 + jnp.exp(-gate)) * up).astype(jnp.bfloat16)

    near_act = activate(near[0], near[1])
    far_act = activate(far[0], far[1])
    down_ready()
    for start in range(0, width, CHUNK):
        columns = slice(start, start + CHUNK)
        total = (
            jnp.dot(near_act, near[2][:, columns], preferred_element_type=jnp.float32)
            + jnp.dot(far_act, far[2][:, columns], preferred_element_type=jnp.float32)
        ).astype(jnp.bfloat16)
        for n, out in enumerate(outs):
            out[:, columns] = total[n * piece_rows : (n + 1) * piece_rows]


def first_kernel(count, *refs):
    pieces, weights, stored = refs[:count], refs[count : count + 5], refs[count + 6]
    outs, loaded, arrived = refs[count + 7 : -2], refs[-2], refs[-1]
    fetch = pltpu.make_async_copy(stored, loaded, arrived)
    fetch.start()
    apply_experts(pieces, weights[:3], list(weights[3:]) + [loaded], fetch.wait, outs)


def later_kernel(count, *refs):
    pieces, weights, outs = refs[:count], refs[count : count + 6], refs[count + 6 :]
    apply_experts(pieces, weights[:3], weights[3:], lambda: None, outs)


def run_experts(pieces, weights, stored=None):
    count = len(pieces)
    piece_rows, width = pieces[0].shape
    results = [jax.ShapeDtypeStruct((piece_rows, width), jnp.bfloat16)] * count
    in_specs = in_vmem(count + len(weights))
    operands = [*pieces, *weights]
    scratch = []
    aliases = {}
    kernel = later_kernel
    if stored is not None:
        kernel = first_kernel
        in_specs.append(pl.BlockSpec(memory_space=pltpu.HBM))
        operands.append(stored)
        aliases = {len(operands) - 2: len(results)}
        results.append(jax.ShapeDtypeStruct(stored.shape, stored.dtype))
        scratch.append(pltpu.SemaphoreType.DMA)
    size = sum(w.size for w in weights)
    return pl.pallas_call(
        lambda *refs: kernel(count, *refs),
        in_specs=in_specs,
        out_specs=in_vmem(len(results)),
        out_shape=results,
        scratch_shapes=scratch,
        input_output_aliases=aliases,
        compiler_params=pltpu.CompilerParams(vmem_limit_bytes=LIMIT * 2**20),
        cost_estimate=pl.CostEstimate(
            flops=2 * count * piece_rows * size, bytes_accessed=2 * size, transcendentals=0
        ),
        name="experts",
    )(*operands)


def spread_kernel(first_slot, count, *refs):
    weigh_ref, pieces, refs = refs[0], refs[1 : 1 + count], refs[1 + count :]
    half = weigh_ref.shape[0] // 2
    piece_rows, width = pieces[0].shape
    slots = slice(first_slot, first_slot + count * piece_rows)
    outs = refs if first_slot == 0 else refs[1:]
    for start in range(0, width, CHUNK):
        columns = slice(start, start + CHUNK)
        rows = jnp.concatenate([p[:, columns] for p in pieces], axis=0)
        both = jnp.dot(weigh_ref[:, slots], rows, preferred_element_type=jnp.float32)
        total = both[:half] + both[half:]
        if first_slot > 0:
            total = (total + refs[0][:, columns]).astype(jnp.bfloat16)
        for n, out in enumerate(outs):
            out[:, columns] = total[n * out.shape[0] : (n + 1) * out.shape[0]]


def spread(weights, pieces, begun=None):
    slots, width = pieces[0].shape
    rows = weights.shape[0] // 2
    first_slot = 0 if begun is None else EARLY * slots
    results = [jax.ShapeDtypeStruct((rows, width), jnp.float32)]
    operands = [weights, *pieces]
    if begun is not None:
        results = [jax.ShapeDtypeStruct((rows // LINE, width), jnp.bfloat16)] * LINE
        operands.append(begun)
    return pl.pallas_call(
        lambda *refs: spread_kernel(first_slot, len(pieces), *refs),
        in_specs=in_vmem(len(operands)),
        out_specs=in_vmem(len(results)),
        out_shape=results,
        compiler_params=pltpu.CompilerParams(vmem_limit_bytes=LIMIT * 2**20),
        cost_estimate=pl.CostEstimate(
            flops=2 * 2 * rows * len(pieces) * slots * width,
            bytes_accessed=2 * width * (len(pieces) * slots + 2 * rows),
            transcendentals=0,
        ),
        name="spread_slots",
    )(*operands)


def add_kernel(parts, *refs):
    pieces, outs = refs[:LINE], refs[LINE:]
    total = pieces[0][...].astype(jnp.float32)
    for piece in pieces[1:]:
        total = total + piece[...].astype(jnp.float32)
    count = outs[0].shape[0]
    for n in range(parts):
        outs[n][...] = total[n * count : (n + 1) * count].astype(jnp.bfloat16)


def add(pieces, parts):
    rows, width = pieces[0].shape
    return pl.pallas_call(
        lambda *refs: add_kernel(parts, *refs),
        in_specs=in_vmem(LINE),
        out_specs=in_vmem(parts),
        out_shape=[jax.ShapeDtypeStruct((rows // parts, width), jnp.bfloat16)] * parts,
        compiler_params=pltpu.CompilerParams(vmem_limit_bytes=LIMIT * 2**20),
        cost_estimate=pl.CostEstimate(
            flops=LINE * rows * width,
            bytes_accessed=2 * (LINE + 1) * rows * width,
            transcendentals=0,
        ),
        name="add_pieces",
    )(*pieces)


def attend(queries, latent_cache, lengths):
    scores = (
        jnp.einsum("rhk,rck->rhc", queries, latent_cache, preferred_element_type=jnp.float32)
        * score_scale
    )
    in_range = jnp.arange(latent_cache.shape[1])[None, None, :] < lengths[:, None, None]
    scores = jnp.where(in_range, scores, -jnp.inf)
    row_max = jnp.max(scores, axis=-1, keepdims=True)
    raised = jnp.exp(scores - row_max)
    probs = (raised / jnp.sum(raised, axis=-1, keepdims=True)).astype(jnp.bfloat16)
    attended = jnp.einsum(
        "rhc,rcl->rhl", probs, latent_cache[:, :, :LAT], preferred_element_type=jnp.float32
    )
    return attended.astype(jnp.bfloat16)


FIRST = ("y", "x")
SECOND = ("x", "z")
THIRD = ("z", "y")


def target_experts():
    zl, zh, x, y, core = [lax.axis_index(axis) for axis in AXES]
    z = zh * 2 + zl
    found = []
    for step in STEPS:
        to_z = jnp.where(core == 0, (z + step) % LINE, z)
        to_y = jnp.where(core == 0, y, (y + step) % LINE)
        found.append((((to_z % 2) * 2 + to_z // 2) * 4 + x) * 2 + to_y // 2)
    return jnp.stack(found).astype(jnp.int32)


def gather_line(rows, axes):
    return [rows] + [shift(rows, axes, step) for step in STEPS[1:]]


def hand_out(pieces, axes):
    return [pieces[0]] + [shift(p, axes, step) for p, step in zip(pieces[1:], STEPS[1:])]


def hand_back(piece, axes, step):
    return shift(piece, axes, -step)


def shards(
    hidden, norm_gain, routes, gate_values, w_gate, w_up, w_down, queries, latent_cache, lengths
):
    tok_rows, topk = routes.shape
    experts = target_experts()
    own = normalize(hidden, norm_gain, routes, gate_values)
    own, w_gate, w_up = lax.optimization_barrier((own, w_gate, w_up))
    far_gate, far_up = to_other_core(w_gate), to_other_core(w_up)
    line = jnp.concatenate(gather_line(own, FIRST), axis=0)
    plane = gather_line(line, SECOND)
    plane, w_gate, w_up, far_gate = lax.optimization_barrier((plane, w_gate, w_up, far_gate))
    chosen = select(plane, experts, tok_rows, topk)
    chosen, w_down = lax.optimization_barrier((chosen, w_down))
    slots = hand_out(chosen, THIRD)
    far_down = to_other_core(w_down)
    weights = weigh(plane, experts, tok_rows, topk)
    attn_out = attend(queries, latent_cache, lengths)

    loaded = load((w_gate, w_up, w_down, far_gate, far_up), w_down.shape)
    group, loaded = lax.optimization_barrier((slots[:EARLY], loaded))
    *results, last = run_experts(group, loaded, far_down)
    group, loaded, last = lax.optimization_barrier((slots[EARLY:], loaded[:5], last))
    results = results + list(run_experts(group, [*loaded, last]))
    back = [results[0]] + [
        hand_back(piece, THIRD, step) for piece, step in zip(results[1:], STEPS[1:])
    ]
    (begun,) = spread(weights, back[:EARLY])
    begun, late = lax.optimization_barrier((begun, back[EARLY:]))
    dense = spread(weights, late, begun)
    dense = [dense[0]] + [
        hand_back(piece, SECOND, step) for piece, step in zip(dense[1:], STEPS[1:])
    ]
    sums = add(dense, LINE)
    sums = [sums[0]] + [hand_back(piece, FIRST, step) for piece, step in zip(sums[1:], STEPS[1:])]
    (moe_out,) = add(sums, 1)
    return (moe_out, attn_out)


def solution(mesh):
    fine = Mesh(mesh.devices.reshape(SIZES), AXES)
    placed = (
        P(AXES, None),
        P(),
        P(AXES, None),
        P(AXES, None),
        P(None, AXES),
        P(None, AXES),
        P(AXES, None),
        P(AXES, None, None),
        P(AXES, None, None),
        P(AXES),
    )
    return jax.shard_map(
        shards,
        mesh=fine,
        in_specs=placed,
        out_specs=(P(AXES, None), P(AXES, None, None)),
        check_vma=False,
    )
```

```python
import itertools

import jax
import jax.numpy as jnp
from jax import lax
from jax.experimental import pallas as pl
from jax.experimental.pallas import tpu as pltpu
from jax.sharding import Mesh, PartitionSpec as P

LAT = 512
CAP = 4

AXES = ("zl", "zh", "x", "y", "core")
SIZES = (2, 2, 4, 4, 2)
LINE = 4
STEPS = (0, 2, 1, -1)
EARLY = 2
META = 128
CHUNK = 1024
LIMIT = 5

norm_eps = 1e-06
score_scale = 0.07216878364870322


def moved_along(place, axis, step):
    place = dict(place)
    if axis == "z":
        z = (place["zh"] * 2 + place["zl"] + step) % LINE
        place["zh"], place["zl"] = z // 2, z % 2
    else:
        place[axis] = (place[axis] + step) % LINE
    return place


def index_of(place):
    index = 0
    for axis, size in zip(AXES, SIZES):
        index = index * size + place[axis]
    return index


def shift(rows, axes, step):
    pairs = []
    for values in itertools.product(*[range(size) for size in SIZES]):
        place = dict(zip(AXES, values))
        pairs.append((index_of(place), index_of(moved_along(place, axes[place["core"]], step))))
    return lax.ppermute(rows, AXES, pairs)


def to_other_core(rows):
    return lax.ppermute(rows, "core", [(0, 1), (1, 0)])


def in_vmem(count):
    return [pl.BlockSpec(memory_space=pltpu.VMEM)] * count


def normalize_kernel(*refs):
    stored, out_ref, held, arrived = refs[:4], refs[4], refs[5:9], refs[9]
    fetches = [
        pltpu.make_async_copy(source, target, arrived.at[n])
        for n, (source, target) in enumerate(zip(stored, held))
    ]
    for fetch in fetches:
        fetch.start()
    for fetch in fetches:
        fetch.wait()
    hidden_ref, gain_ref, routes_ref, gates_ref = held
    features = hidden_ref[...].astype(jnp.float32)
    squares = jnp.mean(features * features, axis=-1, keepdims=True)
    normed = features * lax.rsqrt(squares + norm_eps) * gain_ref[...]
    gates = gates_ref[...]
    high = gates.astype(jnp.bfloat16).astype(jnp.float32)
    tok_rows, topk = gates.shape
    rest = jnp.zeros((tok_rows, META - 3 * topk), jnp.float32)
    meta = jnp.concatenate(
        [routes_ref[...].astype(jnp.float32), high, gates - high, rest], axis=1
    )
    width = hidden_ref.shape[1]
    out_ref[:, :width] = normed.astype(jnp.bfloat16)
    out_ref[:, width:] = meta.astype(jnp.bfloat16)


def normalize(hidden, norm_gain, routes, gate_values):
    tok_rows, width = hidden.shape
    operands = (hidden, norm_gain.reshape(1, -1), routes, gate_values)
    return pl.pallas_call(
        normalize_kernel,
        in_specs=[pl.BlockSpec(memory_space=pltpu.HBM)] * 4,
        out_specs=in_vmem(1)[0],
        out_shape=jax.ShapeDtypeStruct((tok_rows, width + META), jnp.bfloat16),
        scratch_shapes=[pltpu.VMEM(operand.shape, operand.dtype) for operand in operands]
        + [pltpu.SemaphoreType.DMA((4,))],
        name="normalize",
    )(*operands)


def slot_table(meta, experts_ref, tok_rows, topk):
    rows = meta.shape[0]
    slots = rows // tok_rows * CAP
    shape = (rows, LINE * slots)
    row = lax.broadcasted_iota(jnp.int32, shape, 0)
    slot = lax.broadcasted_iota(jnp.int32, shape, 1)
    which = lax.broadcasted_iota(jnp.int32, (1, LINE * slots), 1) // slots
    expert = jnp.zeros(which.shape, jnp.int32)
    for n in range(LINE):
        expert = jnp.where(which == n, experts_ref[n], expert)
    expert = expert.astype(jnp.float32)
    named = jnp.zeros(shape, jnp.float32)
    high = jnp.zeros(shape, jnp.float32)
    low = jnp.zeros(shape, jnp.float32)
    for k in range(topk):
        hit = meta[:, k : k + 1] == expert
        named = jnp.where(hit, 1.0, named)
        high = jnp.where(hit, meta[:, topk + k : topk + k + 1], high)
        low = jnp.where(hit, meta[:, 2 * topk + k : 2 * topk + k + 1], low)
    to = lax.broadcasted_iota(jnp.int32, (rows, rows), 0)
    frm = lax.broadcasted_iota(jnp.int32, (rows, rows), 1)
    before = ((to // tok_rows == frm // tok_rows) & (frm < to)).astype(jnp.float32)
    rank = jnp.dot(
        before.astype(jnp.bfloat16), named.astype(jnp.bfloat16), preferred_element_type=jnp.float32
    )
    place = slot % slots
    fills = (
        (named > 0.5)
        & (row // tok_rows == place // CAP)
        & (rank == (place % CAP).astype(jnp.float32))
    )
    return fills, jnp.where(fills, high, 0.0), jnp.where(fills, low, 0.0)


def select_kernel(tok_rows, topk, experts_ref, *refs):
    pieces, outs = refs[:LINE], refs[LINE:]
    width = outs[0].shape[1]
    slots = outs[0].shape[0]
    meta = jnp.concatenate([p[:, width:] for p in pieces], axis=0).astype(jnp.float32)
    fills, _, _ = slot_table(meta, experts_ref, tok_rows, topk)
    pick = fills.astype(jnp.float32).astype(jnp.bfloat16)
    for start in range(0, width, CHUNK):
        columns = slice(start, start + CHUNK)
        rows = jnp.concatenate([p[:, columns] for p in pieces], axis=0)
        picked = lax.dot_general(
            pick, rows, (((0,), (0,)), ((), ())), preferred_element_type=jnp.float32
        ).astype(jnp.bfloat16)
        for n in range(LINE):
            outs[n][:, columns] = picked[n * slots : (n + 1) * slots]


def select(pieces, experts, tok_rows, topk):
    piece_rows = pieces[0].shape[0]
    width = pieces[0].shape[1] - META
    slots = LINE * piece_rows // tok_rows * CAP
    return pl.pallas_call(
        lambda *refs: select_kernel(tok_rows, topk, *refs),
        in_specs=[pl.BlockSpec(memory_space=pltpu.SMEM)] + in_vmem(LINE),
        out_specs=in_vmem(LINE),
        out_shape=[jax.ShapeDtypeStruct((slots, width), jnp.bfloat16)] * LINE,
        compiler_params=pltpu.CompilerParams(vmem_limit_bytes=LIMIT * 2**20),
        cost_estimate=pl.CostEstimate(
            flops=2 * LINE * slots * LINE * piece_rows * width,
            bytes_accessed=2 * LINE * width * (slots + piece_rows),
            transcendentals=0,
        ),
        name="select_slots",
    )(experts, *pieces)


def weigh_kernel(tok_rows, topk, experts_ref, *refs):
    metas, weigh_ref = refs[:LINE], refs[LINE]
    meta = jnp.concatenate([m[:, -META:] for m in metas], axis=0).astype(jnp.float32)
    _, high, low = slot_table(meta, experts_ref, tok_rows, topk)
    weigh_ref[...] = jnp.concatenate([high, low], axis=0).astype(jnp.bfloat16)


def weigh(pieces, experts, tok_rows, topk):
    piece_rows = pieces[0].shape[0]
    rows = LINE * piece_rows
    slots = rows // tok_rows * CAP
    return pl.pallas_call(
        lambda *refs: weigh_kernel(tok_rows, topk, *refs),
        in_specs=[pl.BlockSpec(memory_space=pltpu.SMEM)] + in_vmem(LINE),
        out_specs=in_vmem(1)[0],
        out_shape=jax.ShapeDtypeStruct((2 * rows, LINE * slots), jnp.bfloat16),
        compiler_params=pltpu.CompilerParams(vmem_limit_bytes=LIMIT * 2**20),
        name="slot_weights",
    )(experts, *pieces)


def load_kernel(count, *refs):
    stored, loaded, arrived = refs[:count], refs[count : 2 * count], refs[-1]
    fetches = [
        pltpu.make_async_copy(source, target, arrived.at[n])
        for n, (source, target) in enumerate(zip(stored, loaded))
    ]
    for fetch in fetches:
        fetch.start()
    for fetch in fetches:
        fetch.wait()


def load(weights, room):
    count = len(weights)
    shapes = [w.shape for w in weights] + [room]
    return pl.pallas_call(
        lambda *refs: load_kernel(count, *refs),
        in_specs=[pl.BlockSpec(memory_space=pltpu.HBM)] * count,
        out_specs=in_vmem(count + 1),
        out_shape=[jax.ShapeDtypeStruct(shape, jnp.bfloat16) for shape in shapes],
        scratch_shapes=[pltpu.SemaphoreType.DMA((count,))],
        compiler_params=pltpu.CompilerParams(vmem_limit_bytes=LIMIT * 2**20),
        cost_estimate=pl.CostEstimate(
            flops=600 * sum(w.size for w in weights), bytes_accessed=0, transcendentals=0
        ),
        name="load_weights",
    )(*weights)


def apply_experts(pieces, near, far, down_ready, outs):
    rows = jnp.concatenate([piece[...] for piece in pieces], axis=0)
    piece_rows, width = pieces[0].shape

    def activate(gates, ups):
        gate = jnp.dot(rows, gates[...], preferred_element_type=jnp.float32)
        up = jnp.dot(rows, ups[...], preferred_element_type=jnp.float32)
        return (gate / (1.0 + jnp.exp(-gate)) * up).astype(jnp.bfloat16)

    near_act = activate(near[0], near[1])
    far_act = activate(far[0], far[1])
    down_ready()
    for start in range(0, width, CHUNK):
        columns = slice(start, start + CHUNK)
        total = (
            jnp.dot(near_act, near[2][:, columns], preferred_element_type=jnp.float32)
            + jnp.dot(far_act, far[2][:, columns], preferred_element_type=jnp.float32)
        ).astype(jnp.bfloat16)
        for n, out in enumerate(outs):
            out[:, columns] = total[n * piece_rows : (n + 1) * piece_rows]


def first_kernel(count, *refs):
    pieces, weights, stored = refs[:count], refs[count : count + 5], refs[count + 6]
    outs, loaded, arrived = refs[count + 7 : -2], refs[-2], refs[-1]
    fetch = pltpu.make_async_copy(stored, loaded, arrived)
    fetch.start()
    apply_experts(pieces, weights[:3], list(weights[3:]) + [loaded], fetch.wait, outs)


def later_kernel(count, *refs):
    pieces, weights, outs = refs[:count], refs[count : count + 6], refs[count + 6 :]
    apply_experts(pieces, weights[:3], weights[3:], lambda: None, outs)


def run_experts(pieces, weights, stored=None):
    count = len(pieces)
    piece_rows, width = pieces[0].shape
    results = [jax.ShapeDtypeStruct((piece_rows, width), jnp.bfloat16)] * count
    in_specs = in_vmem(count + len(weights))
    operands = [*pieces, *weights]
    scratch = []
    aliases = {}
    kernel = later_kernel
    if stored is not None:
        kernel = first_kernel
        in_specs.append(pl.BlockSpec(memory_space=pltpu.HBM))
        operands.append(stored)
        aliases = {len(operands) - 2: len(results)}
        results.append(jax.ShapeDtypeStruct(stored.shape, stored.dtype))
        scratch.append(pltpu.SemaphoreType.DMA)
    size = sum(w.size for w in weights)
    return pl.pallas_call(
        lambda *refs: kernel(count, *refs),
        in_specs=in_specs,
        out_specs=in_vmem(len(results)),
        out_shape=results,
        scratch_shapes=scratch,
        input_output_aliases=aliases,
        compiler_params=pltpu.CompilerParams(vmem_limit_bytes=LIMIT * 2**20),
        cost_estimate=pl.CostEstimate(
            flops=2 * count * piece_rows * size, bytes_accessed=2 * size, transcendentals=0
        ),
        name="experts",
    )(*operands)


def spread_kernel(first_slot, count, *refs):
    weigh_ref, pieces, refs = refs[0], refs[1 : 1 + count], refs[1 + count :]
    half = weigh_ref.shape[0] // 2
    piece_rows, width = pieces[0].shape
    slots = slice(first_slot, first_slot + count * piece_rows)
    outs = refs if first_slot == 0 else refs[1:]
    for start in range(0, width, CHUNK):
        columns = slice(start, start + CHUNK)
        rows = jnp.concatenate([p[:, columns] for p in pieces], axis=0)
        both = jnp.dot(weigh_ref[:, slots], rows, preferred_element_type=jnp.float32)
        total = both[:half] + both[half:]
        if first_slot > 0:
            total = (total + refs[0][:, columns]).astype(jnp.bfloat16)
        for n, out in enumerate(outs):
            out[:, columns] = total[n * out.shape[0] : (n + 1) * out.shape[0]]


def spread(weights, pieces, begun=None):
    slots, width = pieces[0].shape
    rows = weights.shape[0] // 2
    first_slot = 0 if begun is None else EARLY * slots
    results = [jax.ShapeDtypeStruct((rows, width), jnp.float32)]
    operands = [weights, *pieces]
    if begun is not None:
        results = [jax.ShapeDtypeStruct((rows // LINE, width), jnp.bfloat16)] * LINE
        operands.append(begun)
    return pl.pallas_call(
        lambda *refs: spread_kernel(first_slot, len(pieces), *refs),
        in_specs=in_vmem(len(operands)),
        out_specs=in_vmem(len(results)),
        out_shape=results,
        compiler_params=pltpu.CompilerParams(vmem_limit_bytes=LIMIT * 2**20),
        cost_estimate=pl.CostEstimate(
            flops=2 * 2 * rows * len(pieces) * slots * width,
            bytes_accessed=2 * width * (len(pieces) * slots + 2 * rows),
            transcendentals=0,
        ),
        name="spread_slots",
    )(*operands)


def add_kernel(parts, *refs):
    pieces, outs = refs[:LINE], refs[LINE:]
    total = pieces[0][...].astype(jnp.float32)
    for piece in pieces[1:]:
        total = total + piece[...].astype(jnp.float32)
    count = outs[0].shape[0]
    for n in range(parts):
        outs[n][...] = total[n * count : (n + 1) * count].astype(jnp.bfloat16)


def add(pieces, parts):
    rows, width = pieces[0].shape
    return pl.pallas_call(
        lambda *refs: add_kernel(parts, *refs),
        in_specs=in_vmem(LINE),
        out_specs=in_vmem(parts),
        out_shape=[jax.ShapeDtypeStruct((rows // parts, width), jnp.bfloat16)] * parts,
        compiler_params=pltpu.CompilerParams(vmem_limit_bytes=LIMIT * 2**20),
        cost_estimate=pl.CostEstimate(
            flops=LINE * rows * width,
            bytes_accessed=2 * (LINE + 1) * rows * width,
            transcendentals=0,
        ),
        name="add_pieces",
    )(*pieces)


def attend(queries, latent_cache, lengths):
    scores = (
        jnp.einsum("rhk,rck->rhc", queries, latent_cache, preferred_element_type=jnp.float32)
        * score_scale
    )
    in_range = jnp.arange(latent_cache.shape[1])[None, None, :] < lengths[:, None, None]
    scores = jnp.where(in_range, scores, -jnp.inf)
    row_max = jnp.max(scores, axis=-1, keepdims=True)
    raised = jnp.exp(scores - row_max)
    probs = (raised / jnp.sum(raised, axis=-1, keepdims=True)).astype(jnp.bfloat16)
    attended = jnp.einsum(
        "rhc,rcl->rhl", probs, latent_cache[:, :, :LAT], preferred_element_type=jnp.float32
    )
    return attended.astype(jnp.bfloat16)


FIRST = ("y", "x")
SECOND = ("x", "z")
THIRD = ("z", "y")


def target_experts():
    zl, zh, x, y, core = [lax.axis_index(axis) for axis in AXES]
    z = zh * 2 + zl
    found = []
    for step in STEPS:
        to_z = jnp.where(core == 0, (z + step) % LINE, z)
        to_y = jnp.where(core == 0, y, (y + step) % LINE)
        found.append((((to_z % 2) * 2 + to_z // 2) * 4 + x) * 2 + to_y // 2)
    return jnp.stack(found).astype(jnp.int32)


def gather_line(rows, axes):
    return [rows] + [shift(rows, axes, step) for step in STEPS[1:]]


def hand_out(pieces, axes):
    return [pieces[0]] + [shift(p, axes, step) for p, step in zip(pieces[1:], STEPS[1:])]


def hand_back(piece, axes, step):
    return shift(piece, axes, -step)


def shards(
    hidden, norm_gain, routes, gate_values, w_gate, w_up, w_down, queries, latent_cache, lengths
):
    tok_rows, topk = routes.shape
    experts = target_experts()
    own = normalize(hidden, norm_gain, routes, gate_values)
    own, w_gate, w_up = lax.optimization_barrier((own, w_gate, w_up))
    far_gate, far_up = to_other_core(w_gate), to_other_core(w_up)
    line = jnp.concatenate(gather_line(own, FIRST), axis=0)
    plane = gather_line(line, SECOND)
    plane, w_gate, w_up, far_gate = lax.optimization_barrier((plane, w_gate, w_up, far_gate))
    chosen = select(plane, experts, tok_rows, topk)
    chosen, w_down = lax.optimization_barrier((chosen, w_down))
    slots = hand_out(chosen, THIRD)
    far_down = to_other_core(w_down)
    weights = weigh(plane, experts, tok_rows, topk)
    attn_out = attend(queries, latent_cache, lengths)

    loaded = load((w_gate, w_up, w_down, far_gate, far_up), w_down.shape)
    group, loaded = lax.optimization_barrier((slots[:EARLY], loaded))
    *results, last = run_experts(group, loaded, far_down)
    group, loaded, last = lax.optimization_barrier((slots[EARLY:], loaded[:5], last))
    results = results + list(run_experts(group, [*loaded, last]))
    back = [results[0]] + [
        hand_back(piece, THIRD, step) for piece, step in zip(results[1:], STEPS[1:])
    ]
    (begun,) = spread(weights, back[:EARLY])
    begun, late = lax.optimization_barrier((begun, back[EARLY:]))
    dense = spread(weights, late, begun)
    dense = [dense[0]] + [
        hand_back(piece, SECOND, step) for piece, step in zip(dense[1:], STEPS[1:])
    ]
    sums = add(dense, LINE)
    sums = [sums[0]] + [hand_back(piece, FIRST, step) for piece, step in zip(sums[1:], STEPS[1:])]
    (moe_out,) = add(sums, 1)
    return (moe_out, attn_out)


def solution(mesh):
    fine = Mesh(mesh.devices.reshape(SIZES), AXES)
    placed = (
        P(AXES, None),
        P(),
        P(AXES, None),
        P(AXES, None),
        P(None, AXES),
        P(None, AXES),
        P(AXES, None),
        P(AXES, None, None),
        P(AXES, None, None),
        P(AXES),
    )
    return jax.shard_map(
        shards,
        mesh=fine,
        in_specs=placed,
        out_specs=(P(AXES, None), P(AXES, None, None)),
        check_vma=False,
    )
```
